32 devices in a mesh: section: 4 (over y, core), dp: 8 (over z, x).
Axes of the slice: x: 2, y: 2, z: 4, core: 2. Of those that a mesh axis runs over, the one named last changes fastest.
Arguments:
- tokens: bfloat16 [1024, 8192], P('dp'), may hold values from -6 to 6
- cotangent: bfloat16 [1024, 8192], P('dp'), may hold values from -9 to 9
- down_weight: bfloat16 [4, 8192, 256], P('section', 'dp'), may hold values from -0.0625 to 0.0625
- up_weight: bfloat16 [4, 8192, 256], P('section', 'dp'), may hold values from -0.0625 to 0.0625
- norm_gain: float32 [4, 8192], P('section'), may hold values from 0.5 to 1.5
- lengths: int32 [8, 4], P('dp'), may hold values from 1 to 96, 128 in all within a row
Outputs:
- fisher: float32 [4, 8192, 256], P('section', 'dp')
The draws below stay inside these ranges and needn't reach their ends.
Inputs may be any that keep to these rules, and one draw needn't show every extreme that they name: Each replica's 4 lengths sum to 128, and the longest in each replica is exactly 96.
All inputs are finite; a program needn't handle non-finite values.
Results may differ from the reference program's by a relative error of at most 0.0039.
Values may be sent and summed in bfloat16 or wider, within the bound.
No kernel may reach another device: no remote copies, remote signals or barrier semaphores. Data moves between devices by JAX's collectives and lax.ppermute only.
A program may use at most 64 MiB of HBM per device.

```python
import math
import jax
import jax.numpy as jnp
import numpy as np
from jax import lax

D = 8192
R = 256
TOK_DEV = 128
SEQ_DEV = 4
MAXLEN = 96
SECTIONS = 4
TOKENS = 1024
N_DP = 8


def level_of(stream_key, dims, split, low, high):
    level = 1.0
    for position, blocks in split:
        draws = jax.random.uniform(jax.random.fold_in(jax.random.fold_in(stream_key, 6), position), (blocks,), jnp.float32, low / len(split), high / len(split))
        level = level * jnp.repeat(jnp.exp(draws), dims[position] // blocks).reshape((-1,) + (1,) * (len(dims) - 1 - position))
    return level


def profile(number_of, total, reach, slope):
    portions = [(1 << 20) // math.isqrt(rank ** slope) + 1 for rank in range(2, number_of + 1)]
    rest, holding = total - reach - (number_of - 1), [1] * (number_of - 1)
    while rest > 0:
        movable = [i for i in range(number_of - 1) if holding[i] < reach]
        whole, remaining = sum([portions[i] for i in movable]), rest
        for i in movable:
            extra = min(reach - holding[i], max(1, remaining * portions[i] // whole), rest)
            holding[i] = holding[i] + extra
            rest = rest - extra
    return np.array([reach] + holding)


def uneven_parts(own_key, number_of, total, bound, lean):
    if number_of == 2:
        one = jax.random.randint(own_key, (), max(1, total - bound), min(bound, total - 1) + 1)
        return jnp.stack([one, total - one])
    sizes = jnp.asarray(profile(number_of, total, bound, lean), jnp.int32)
    twos = (number_of - 1) // 2
    source_of, taker = sizes[1:1 + 2 * twos:2], sizes[2:2 + 2 * twos:2]
    room = jnp.minimum(source_of - 1, bound - taker)
    moved = jax.random.randint(jax.random.fold_in(own_key, 1), (twos,), 0, 1 << 20) % (room + 1)
    sizes = sizes.at[1:1 + 2 * twos:2].set(source_of - moved).at[2:2 + 2 * twos:2].set(taker + moved)
    return sizes[jax.random.permutation(jax.random.fold_in(own_key, 2), number_of)]


def bell_draw(key, extent, spread, reach, shards=(), kind=jnp.bfloat16):
    result = spread * jax.random.normal(key, extent, jnp.float32)
    if shards:
        result = result * level_of(key, extent, shards, -0.22, 0.18)
    return jnp.clip(result, -reach, reach).astype(kind)


def setup_inputs(seed: int = 0) -> dict:
    keys = jax.random.split(jax.random.key(seed), 7)
    tokens = bell_draw(keys[0], (TOKENS, D), 1.0, 6.0, ((0, 8),))
    cotangent = bell_draw(keys[1], (TOKENS, D), 1.5, 9.0, ((0, 8),))
    down_weight = bell_draw(keys[2], (SECTIONS, D, R), D ** -0.5, 0.0625, ((0, 4), (1, 8)))
    up_weight = bell_draw(keys[3], (SECTIONS, D, R), D ** -0.5, 0.0625, ((0, 4), (1, 8)))
    norm_gain = jnp.clip(1.0 + 0.1 * jax.random.normal(keys[4], (SECTIONS, D), jnp.float32), 0.5, 1.5)
    lengths = jax.vmap(lambda own: uneven_parts(own, SEQ_DEV, TOK_DEV, MAXLEN, 2))(jax.random.split(keys[5], N_DP)).reshape((N_DP, SEQ_DEV)).astype(jnp.int32)
    return {"tokens": tokens, "cotangent": cotangent, "down_weight": down_weight, "up_weight": up_weight, "norm_gain": norm_gain, "lengths": lengths}


epsilon = 1e-05

def layer_forward(inputs, gain_row, w_down, w_up):
    wide_rows = inputs.astype(jnp.float32)
    inverse_rms = lax.rsqrt(lax.optimization_barrier(jnp.mean(wide_rows * wide_rows, axis=-1, keepdims=True)) + epsilon)
    normed = (wide_rows * inverse_rms * gain_row).astype(jnp.bfloat16)
    pre_act = jnp.dot(normed, w_down, preferred_element_type=jnp.float32)
    activated = jax.nn.silu(pre_act).astype(jnp.bfloat16)
    branch = lax.dot_general(activated, w_up, (((1,), (1,)), ((), ())), preferred_element_type=jnp.float32)
    return (wide_rows + branch).astype(jnp.bfloat16)

def layer_backward(inputs, upstream, gain_row, w_down, w_up):
    wide_rows = inputs.astype(jnp.float32)
    inverse_rms = lax.rsqrt(lax.optimization_barrier(jnp.mean(wide_rows * wide_rows, axis=-1, keepdims=True)) + epsilon)
    normed = (wide_rows * inverse_rms * gain_row).astype(jnp.bfloat16)
    pre_act = jnp.dot(normed, w_down, preferred_element_type=jnp.float32)
    act_grad = jnp.dot(upstream, w_up, preferred_element_type=jnp.float32)
    sigmoid_z = jax.nn.sigmoid(pre_act)
    pre_grad = (act_grad * sigmoid_z * (1.0 + pre_act * (1.0 - sigmoid_z))).astype(jnp.bfloat16)
    norm_grad = lax.dot_general(pre_grad, w_down, (((1,), (1,)), ((), ())), preferred_element_type=jnp.float32)
    gained = norm_grad * gain_row
    inner = lax.optimization_barrier(jnp.mean(wide_rows * gained, axis=-1, keepdims=True))
    input_grad = upstream.astype(jnp.float32) + inverse_rms * (gained - wide_rows * inverse_rms * inverse_rms * inner)
    return (input_grad.astype(jnp.bfloat16), normed, pre_grad)

def fisher_block(normed, pre_grad, lengths):
    offsets = jnp.cumsum(lengths, axis=1) - lengths + (jnp.arange(N_DP, dtype=jnp.int32) * TOK_DEV)[:, None]
    begins = offsets.reshape(-1).astype(jnp.int32)
    counts = lengths.reshape(-1).astype(jnp.int32)
    padded_norm = jnp.concatenate([normed, jnp.zeros((MAXLEN, D), normed.dtype)], axis=0)
    padded_grad = jnp.concatenate([pre_grad, jnp.zeros((MAXLEN, R), pre_grad.dtype)], axis=0)

    def accumulate(fisher_sum, item):
        begin_row, seq_length = item
        window_norm = lax.dynamic_slice_in_dim(padded_norm, begin_row, MAXLEN, 0)
        window_grad = lax.dynamic_slice_in_dim(padded_grad, begin_row, MAXLEN, 0)
        live_rows = jnp.arange(MAXLEN, dtype=jnp.int32) < seq_length
        window_grad = jnp.where(live_rows[:, None], window_grad, jnp.zeros_like(window_grad))
        seq_grad = lax.dot_general(window_norm, window_grad, (((0,), (0,)), ((), ())), preferred_element_type=jnp.float32)
        return (fisher_sum + seq_grad * seq_grad, None)
    fisher_sum = lax.scan(accumulate, jnp.zeros((D, R), jnp.float32), (begins, counts))[0]
    return fisher_sum / TOKENS

def reference(tokens, cotangent, down_weight, up_weight, norm_gain, lengths):
    hidden = tokens
    layer_inputs = []
    for layer_index in range(SECTIONS):
        layer_inputs.append(hidden)
        hidden = layer_forward(hidden, norm_gain[layer_index], down_weight[layer_index], up_weight[layer_index])
    upstream = cotangent
    blocks = [None] * SECTIONS
    for layer_index in reversed(range(SECTIONS)):
        upstream, normed, pre_grad = layer_backward(layer_inputs[layer_index], upstream, norm_gain[layer_index], down_weight[layer_index], up_weight[layer_index])
        blocks[layer_index] = fisher_block(normed, pre_grad, lengths)
    return jnp.stack(blocks)
```

```python
import functools

import jax
import jax.numpy as jnp
from jax import lax
from jax.experimental import pallas as pl
from jax.experimental.pallas import tpu as pltpu
from jax.sharding import PartitionSpec as P

epsilon = 1e-05
bf16 = jnp.bfloat16
f32 = jnp.float32
VMEM_BYTES = 56 * 1024 * 1024


def dot(a, b, ca, cb):
    return lax.dot_general(a, b, (((ca,), (cb,)), ((), ())), preferred_element_type=f32)


def core_swap(x):
    count = lax.axis_size("section")
    return lax.ppermute(x, "section", [(i, i ^ 1) for i in range(count)])


def chip_shift(x, by):
    count = lax.axis_size("section")
    return lax.ppermute(x, "section", [(i, (i - 2 * by) % count) for i in range(count)])


def section_order():
    count = lax.axis_size("section")
    me = lax.axis_index("section")
    same = [(me + 2 * j) % count for j in range(count // 2)]
    other = [((me ^ 1) + 2 * j) % count for j in range(count // 2)]
    return jnp.stack(same + other).astype(jnp.int32)


def gather_section(x):
    count = lax.axis_size("section")
    same = [x] + [chip_shift(x, j) for j in range(1, count // 2)]
    return same + [core_swap(b) for b in same]


def spread(x):
    peers = lax.axis_size("dp")
    return lax.all_to_all(jnp.broadcast_to(x[None], (peers,) + x.shape), "dp", 0, 0, tiled=True)


def gram_pairs(count):
    mixed = [(k, l) for l in range(count) for k in range(l)]
    ups = [(k, count + j) for j in range(count - 1) for k in range(j + 1)]
    return mixed + ups


def project_kernel(count, order, left, right, rows_ref, *refs):
    weights = refs[:count]
    part_ref, gram_ref, table = refs[count:]
    peers, _, t, width = rows_ref.shape
    r = table.shape[2]
    for i in range(count):
        table[order[i]] = weights[i][:, :r]
        table[count + order[i]] = weights[i][:, r:]
    x = rows_ref[:, 0].reshape(peers * t, width)
    c = rows_ref[:, 1].reshape(peers * t, width)
    for m in range(3 * count - 1):
        if m < 2 * count - 1:
            out = dot(x, table[m], 1, 0)
        else:
            out = dot(c, table[m - count + 1], 1, 0)
        part_ref[:, m] = out.astype(bf16).reshape(peers, t, r)
    for p in range(count - 1):
        gram_ref[p] = dot(table[count + left[p]], table[right[p]], 0, 0).astype(bf16)


def recur_kernel(count, width, order, sums_ref, sq_ref, *refs):
    grams = refs[:count]
    out_ref, table = refs[count:]
    per = count - 1
    for i in range(count):
        for p in range(per):
            table[order[i] * per + p] = grams[i][p]
    place = {pair: n for n, pair in enumerate(gram_pairs(count))}

    def mixed(k, l):
        return table[place[(k, l)]]

    def ups(k, j, a):
        if k <= j:
            return dot(a, table[place[(k, count + j)]], 1, 0)
        return dot(a, table[place[(j, count + k)]], 1, 1)

    total = jnp.sum(sums_ref[...].astype(f32), axis=0)
    proj = [total[l] for l in range(count)]
    hu = [total[count + k] for k in range(count - 1)]
    back = [total[2 * count - 1 + l] for l in range(count)]
    norm = sq_ref[...]
    invs, pres, hus = [], [], []
    for l in range(count):
        inv = lax.rsqrt(norm / width + epsilon)
        pre = inv * proj[l]
        invs.append(inv)
        pres.append(pre)
        hus.append(list(hu))
        if l < count - 1:
            act = (pre * jax.nn.sigmoid(pre)).astype(bf16)
            out_ref[count + l] = act
            wide = act.astype(f32)
            for j in range(l + 1, count):
                proj[j] = proj[j] + dot(act, mixed(l, j), 1, 0)
            step = [ups(l, j, act) for j in range(count - 1)]
            norm = norm + jnp.sum(wide * (2.0 * hu[l] + step[l]), axis=-1, keepdims=True)
            hu = [hu[j] + step[j] for j in range(count - 1)]
    for l in reversed(range(count)):
        s = jax.nn.sigmoid(pres[l])
        grad = (back[l] * s * (1.0 + pres[l] * (1.0 - s))).astype(bf16)
        wide = grad.astype(f32)
        out_ref[l] = (wide * invs[l]).astype(bf16)
        inner = jnp.sum(wide * proj[l], axis=-1, keepdims=True) / width
        for j in range(l):
            back[j] = back[j] + invs[l] * (
                dot(grad, mixed(j, l), 1, 1) - invs[l] * invs[l] * inner * hus[l][j]
            )


def fisher_kernel(count, seqs, scale, order, me, *refs):
    rows = refs[:count]
    weights = refs[count : 2 * count]
    same_ref, other_ref, seg_ref, gain_ref, out_ref, acc = refs[2 * count :]
    n = pl.program_id(0)
    half = count // 2
    t = rows[0].shape[1]
    r = out_ref.shape[1]
    width = out_ref.shape[0]

    def column(m):
        parts = [same_ref[0, j, m] for j in range(half)] + [other_ref[0, j, m] for j in range(half)]
        return jnp.concatenate(parts, axis=0)

    h = jnp.concatenate([rows[i][0] for i in range(count)], axis=0).astype(f32)
    for i in range(count):
        act = column(2 + jnp.minimum(order[i], count - 2))
        act = jnp.where(order[i] < me[0], act, jnp.zeros_like(act))
        h = h + dot(act, weights[i][:, r:], 1, 1)
    h = h.astype(bf16)
    grad = column(lax.rem(me[0], 2)).astype(f32).T
    seg = seg_ref[0]
    total = jnp.zeros((r, width), f32)
    for q in range(seqs):
        masked = jnp.where(seg == q, grad, 0.0).astype(bf16)
        g = dot(masked, h, 1, 0)
        total = total + g * g

    @pl.when(n == 0)
    def _():
        acc[...] = total

    @pl.when(n > 0)
    def _():
        acc[...] = acc[...] + total

    @pl.when(n == pl.num_programs(0) - 1)
    def _():
        gain = gain_ref[...]
        out_ref[...] = (acc[...] * (gain * gain * scale)).T


def per_device(tokens, cotangent, down_weight, up_weight, norm_gain, lengths):
    count = lax.axis_size("section")
    peers = lax.axis_size("dp")
    me = lax.axis_index("section")
    spot = lax.axis_index("dp")
    row_count, width = tokens.shape
    block = width // peers
    t = row_count // count
    r = down_weight.shape[2]
    order = section_order()
    params = pltpu.CompilerParams(vmem_limit_bytes=VMEM_BYTES)
    smem = pl.BlockSpec(memory_space=pltpu.SMEM)
    vmem = pl.BlockSpec(memory_space=pltpu.VMEM)

    gain = lax.dynamic_slice_in_dim(norm_gain[0], spot * block, block, 0)
    gained = (down_weight[0].astype(f32) * gain[:, None]).astype(bf16)
    weights = gather_section(jnp.concatenate([gained, up_weight[0]], axis=1))

    mine = lax.dynamic_slice_in_dim(tokens, me * t, t, 0)
    mine_cot = lax.dynamic_slice_in_dim(cotangent, me * t, t, 0)
    wide = mine.astype(f32)
    square = jnp.sum(wide * wide, axis=-1, keepdims=True)
    both = jnp.stack([mine.reshape(t, peers, block), mine_cot.reshape(t, peers, block)])
    rows = lax.all_to_all(both.transpose(2, 0, 1, 3), "dp", 0, 0, tiled=True)

    pairs = gram_pairs(count)
    left = lax.dynamic_slice_in_dim(jnp.array([a for a, _ in pairs], jnp.int32), me * (count - 1), count - 1)
    right = lax.dynamic_slice_in_dim(jnp.array([b for _, b in pairs], jnp.int32), me * (count - 1), count - 1)
    part, gram = pl.pallas_call(
        functools.partial(project_kernel, count),
        out_shape=(
            jax.ShapeDtypeStruct((peers, 3 * count - 1, t, r), bf16),
            jax.ShapeDtypeStruct((count - 1, r, r), bf16),
        ),
        in_specs=[smem] * 3 + [vmem] * (1 + count),
        out_specs=(vmem, vmem),
        scratch_shapes=[pltpu.VMEM((2 * count, block, r), bf16)],
        compiler_params=params,
        name="project",
    )(order, left, right, rows, *weights)

    line = jnp.zeros((peers, 16, r), bf16).at[:, 0, : lengths.shape[1]].set(lengths.astype(bf16))
    gram_rows = (count - 1) * r // peers
    packed = jnp.concatenate([gram.reshape(peers, gram_rows, r), line], axis=1)
    packed = lax.all_to_all(packed, "dp", 0, 0, tiled=True)
    gram_sum = jnp.sum(packed[:, :gram_rows].astype(f32), axis=0).astype(bf16)
    all_lengths = packed[:, gram_rows, : lengths.shape[1]].astype(jnp.int32)
    sums = lax.all_to_all(part, "dp", 0, 0, tiled=True)
    grams = gather_section(spread(gram_sum).reshape(count - 1, r, r))

    states = pl.pallas_call(
        functools.partial(recur_kernel, count, width),
        out_shape=jax.ShapeDtypeStruct((2 * count - 1, t, r), bf16),
        in_specs=[smem] + [vmem] * (2 + count),
        out_specs=vmem,
        scratch_shapes=[pltpu.VMEM((count * (count - 1), r, r), bf16)],
        compiler_params=params,
        name="recur",
    )(order, sums, square, *grams)

    def wanted_by(other):
        first = lax.dynamic_slice_in_dim(states, other - lax.rem(other, 2), 2, 0)
        return jnp.concatenate([first, states[count:]], axis=0)

    held = [wanted_by(me)]
    for j in range(1, count // 2):
        held.append(chip_shift(wanted_by(lax.rem(me + count - 2 * j, count)), j))
    same = spread(jnp.stack(held))
    other = core_swap(same)
    all_rows = gather_section(rows[:, 0])

    ends = jnp.cumsum(all_lengths, axis=1)
    position = (order[:, None] * t + jnp.arange(t, dtype=jnp.int32)[None]).reshape(-1)
    seg = jnp.sum(position[None, None, :] >= ends[:, :, None], axis=1).astype(jnp.int32)
    seg = seg.reshape(peers, 1, row_count)

    def whole(shape):
        return pl.BlockSpec(shape, lambda n: (0,) * len(shape))

    def step(shape):
        return pl.BlockSpec(shape, lambda n: (n,) + (0,) * (len(shape) - 1))

    fisher = pl.pallas_call(
        functools.partial(fisher_kernel, count, lengths.shape[1], 1.0 / (row_count * peers)),
        grid=(peers,),
        out_shape=jax.ShapeDtypeStruct((block, r), f32),
        in_specs=[smem, smem]
        + [step((1, t, block))] * count
        + [whole((block, 2 * r))] * count
        + [step((1,) + same.shape[1:])] * 2
        + [step((1, 1, row_count)), whole((1, block))],
        out_specs=whole((block, r)),
        scratch_shapes=[pltpu.VMEM((r, block), f32)],
        compiler_params=params,
        name="squares",
    )(order, me.astype(jnp.int32)[None], *all_rows, *weights, same, other, seg, gain[None])
    return fisher[None]


def solution(mesh):
    in_specs = (
        P("dp", None),
        P("dp", None),
        P("section", "dp", None),
        P("section", "dp", None),
        P("section", None),
        P("dp", None),
    )
    out_specs = P("section", "dp", None)
    return jax.shard_map(
        per_device, mesh=mesh, in_specs=in_specs, out_specs=out_specs, check_vma=False
    )
```

```python
import functools

import jax
import jax.numpy as jnp
from jax import lax
from jax.experimental import pallas as pl
from jax.experimental.pallas import tpu as pltpu
from jax.sharding import PartitionSpec as P

epsilon = 1e-05
bf16 = jnp.bfloat16
f32 = jnp.float32
VMEM_BYTES = 56 * 1024 * 1024


def dot(a, b, ca, cb):
    return lax.dot_general(a, b, (((ca,), (cb,)), ((), ())), preferred_element_type=f32)


def core_swap(x):
    count = lax.axis_size("section")
    return lax.ppermute(x, "section", [(i, i ^ 1) for i in range(count)])


def chip_shift(x, by):
    count = lax.axis_size("section")
    return lax.ppermute(x, "section", [(i, (i - 2 * by) % count) for i in range(count)])


def section_order():
    count = lax.axis_size("section")
    me = lax.axis_index("section")
    same = [(me + 2 * j) % count for j in range(count // 2)]
    other = [((me ^ 1) + 2 * j) % count for j in range(count // 2)]
    return jnp.stack(same + other).astype(jnp.int32)


def gather_section(x):
    count = lax.axis_size("section")
    same = [x] + [chip_shift(x, j) for j in range(1, count // 2)]
    return same + [core_swap(b) for b in same]


def spread(x):
    peers = lax.axis_size("dp")
    return lax.all_to_all(jnp.broadcast_to(x[None], (peers,) + x.shape), "dp", 0, 0, tiled=True)


def gram_pairs(count):
    ups = [(k, count + j) for j in range(count - 1) for k in range(j + 1)]
    listed = []
    for chip in range(count // 2):
        own = [(k, l) for l in (2 * chip, 2 * chip + 1) for k in range(l)]
        spare = 2 * (count - 1) - len(own)
        listed += own + ups[:spare]
        ups = ups[spare:]
    return listed


def prepare_kernel(place, tokens_ref, cot_ref, down_ref, gain_ref, rows_ref, cot_rows_ref, square_ref, weight_ref):
    peers, t, block = rows_ref.shape
    r = down_ref.shape[2]
    pieces = block // r
    total = jnp.zeros((t, 1), f32)
    for n in range(peers):
        piece = tokens_ref[:, n * block : (n + 1) * block]
        wide = piece.astype(f32)
        total = total + jnp.sum(wide * wide, axis=-1, keepdims=True)
        rows_ref[n] = piece
        for b in range(pieces):
            start = n * block + b * r
            cot_rows_ref[n, b * t : (b + 1) * t] = cot_ref[:, start : start + r]
    square_ref[...] = total
    gain = gain_ref[...].reshape(block, 1)
    weight_ref[...] = (down_ref[0].astype(f32) * gain).astype(bf16)


def gram_kernel(count, order, left, right, *refs):
    ups = refs[:count]
    mine, partner, gram_ref, table = refs[count:]
    core = lax.rem(order[0], 2)
    table[core] = mine[...]
    table[1 - core] = partner[...]
    for i in range(count):
        table[2 + order[i]] = ups[i][...]
    for p in range(count - 1):
        gram_ref[p] = dot(table[2 + left[p]], table[right[p]], 0, 0).astype(bf16)


def project_kernel(count, room, order, rows_ref, *refs):
    downs = refs[:count]
    ups = refs[count : 2 * count]
    part_ref = refs[2 * count]
    peers, t, width = rows_ref.shape
    r = part_ref.shape[2]
    x = rows_ref[...].reshape(peers * t, width)

    def place(m):
        return pl.ds(pl.multiple_of(room + m * t, t), t)

    for i in range(count):
        layer = order[i]
        out = dot(x, downs[i][...], 1, 0)
        part_ref[:, place(layer), :] = out.astype(bf16).reshape(peers, t, r)

        @pl.when(layer < count - 1)
        def _():
            out = dot(x, ups[i][...], 1, 0)
            part_ref[:, place(count + layer), :] = out.astype(bf16).reshape(peers, t, r)


def project_cot_kernel(count, order, packed_ref, *refs):
    ups = refs[:count]
    part_ref = refs[count]
    peers, rows, r = part_ref.shape
    t = rows // count
    width = ups[0].shape[0]
    c = jnp.concatenate(
        [packed_ref[:, b * t : (b + 1) * t].reshape(peers * t, r) for b in range(width // r)], axis=1
    )
    for i in range(count):
        out = dot(c, ups[i][...], 1, 0)
        start = pl.multiple_of(order[i] * t, t)
        part_ref[:, pl.ds(start, t), :] = out.astype(bf16).reshape(peers, t, r)


def recur_kernel(count, width, room, order, sums_ref, back_ref, sq_ref, *refs):
    grams = refs[:count]
    out_ref, table, grads = refs[count:]
    half, _, t, _ = out_ref.shape
    per = count - 1
    for i in range(count):
        for p in range(per):
            table[order[i] * per + p] = grams[i][p]
    place = {pair: n for n, pair in enumerate(gram_pairs(count))}

    def mixed(k, l):
        return table[place[(k, l)]]

    def ups(k, j, a):
        if k <= j:
            return dot(a, table[place[(k, count + j)]], 1, 0)
        return dot(a, table[place[(j, count + k)]], 1, 1)

    def total(ref, start):
        return jnp.sum(ref[:, start : start + t].astype(f32), axis=0)

    proj = [total(sums_ref, room + l * t) for l in range(count)]
    hu = [total(sums_ref, room + (count + k) * t) for k in range(count - 1)]
    back = [total(back_ref, l * t) for l in range(count)]
    norm = sq_ref[...]
    invs, pres, hus = [], [], []
    for l in range(count):
        inv = lax.rsqrt(norm / width + epsilon)
        pre = inv * proj[l]
        invs.append(inv)
        pres.append(pre)
        hus.append(list(hu))
        if l < count - 1:
            act = (pre * jax.nn.sigmoid(pre)).astype(bf16)
            for j in range(half):
                out_ref[j, 2 + l] = act
            wide = act.astype(f32)
            for j in range(l + 1, count):
                proj[j] = proj[j] + dot(act, mixed(l, j), 1, 0)
            step = [ups(l, j, act) for j in range(count - 1)]
            norm = norm + jnp.sum(wide * (2.0 * hu[l] + step[l]), axis=-1, keepdims=True)
            hu = [hu[j] + step[j] for j in range(count - 1)]
    for l in reversed(range(count)):
        s = jax.nn.sigmoid(pres[l])
        grad = (back[l] * s * (1.0 + pres[l] * (1.0 - s))).astype(bf16)
        wide = grad.astype(f32)
        grads[l] = (wide * invs[l]).astype(bf16)
        inner = jnp.sum(wide * proj[l], axis=-1, keepdims=True) / width
        for j in range(l):
            back[j] = back[j] + invs[l] * (
                dot(grad, mixed(j, l), 1, 1) - invs[l] * invs[l] * inner * hus[l][j]
            )
    chip = order[0] // 2
    for j in range(half):
        other = lax.rem(chip + half - j, half)
        out_ref[j, 0] = grads[2 * other]
        out_ref[j, 1] = grads[2 * other + 1]


def fisher_kernel(count, seqs, scale, order, me, *refs):
    rows = refs[:count]
    ups = refs[count : 2 * count]
    same_ref, other_ref, seg_ref, gain_ref, out_ref, acc, hidden, masks = refs[2 * count :]
    half = count // 2
    peers, t, width = rows[0].shape
    r = out_ref.shape[1]
    chunk = min(r, width)
    span = count * t

    def column(n, m):
        parts = [same_ref[n, j, m] for j in range(half)] + [other_ref[n, j, m] for j in range(half)]
        return jnp.concatenate(parts, axis=0)

    acts = []
    for i in range(1, count):
        act = jnp.concatenate([column(n, 2 + jnp.minimum(order[i], count - 2)) for n in range(peers)], axis=0)
        acts.append(jnp.where(order[i] < me[0], act, jnp.zeros_like(act)))
    for n in range(peers):
        grad = column(n, lax.rem(me[0], 2)).astype(f32).T
        seg = seg_ref[n]
        for q in range(seqs):
            masks[n, q * r : (q + 1) * r] = jnp.where(seg == q, grad, 0.0).astype(bf16)
    for f in range(width // chunk):
        cols = slice(f * chunk, (f + 1) * chunk)
        update = dot(acts[0], ups[1][cols], 1, 1)
        for i in range(2, count):
            update = update + dot(acts[i - 1], ups[i][cols], 1, 1)
        for n in range(peers):
            h = jnp.concatenate([rows[i][n, :, cols] for i in range(count)], axis=0).astype(f32)
            hidden[n] = (h + update[n * span : (n + 1) * span]).astype(bf16)
        for n in range(peers):
            g = dot(masks[n], hidden[n], 1, 0)
            g = g * g
            total = g[:r]
            for q in range(1, seqs):
                total = total + g[q * r : (q + 1) * r]
            if n == 0:
                acc[...] = total
            else:
                acc[...] = acc[...] + total
        gain = gain_ref[:, cols]
        out_ref[cols] = (acc[...] * (gain * gain * scale)).T


def per_device(tokens, cotangent, down_weight, up_weight, norm_gain, lengths):
    count = lax.axis_size("section")
    peers = lax.axis_size("dp")
    me = lax.axis_index("section")
    spot = lax.axis_index("dp")
    row_count, width = tokens.shape
    block = width // peers
    t = row_count // count
    r = down_weight.shape[2]
    order = section_order()
    params = pltpu.CompilerParams(vmem_limit_bytes=VMEM_BYTES)
    smem = pl.BlockSpec(memory_space=pltpu.SMEM)
    vmem = pl.BlockSpec(memory_space=pltpu.VMEM)

    ups = gather_section(up_weight[0])
    token_send, cot_send, square, weight = pl.pallas_call(
        prepare_kernel,
        grid_spec=pltpu.PrefetchScalarGridSpec(
            num_scalar_prefetch=1,
            grid=(1,),
            in_specs=[
                pl.BlockSpec((t, width), lambda n, place: (place[0], 0)),
                pl.BlockSpec((t, width), lambda n, place: (place[0], 0)),
                pl.BlockSpec((1, block, r), lambda n, place: (0, 0, 0)),
                pl.BlockSpec((1, block), lambda n, place: (0, place[1])),
            ],
            out_specs=[
                pl.BlockSpec((peers, t, block), lambda n, place: (0, 0, 0)),
                pl.BlockSpec((peers, t * (block // r), r), lambda n, place: (0, 0, 0)),
                pl.BlockSpec((t, 1), lambda n, place: (0, 0)),
                pl.BlockSpec((block, r), lambda n, place: (0, 0)),
            ],
        ),
        out_shape=(
            jax.ShapeDtypeStruct((peers, t, block), bf16),
            jax.ShapeDtypeStruct((peers, t * (block // r), r), bf16),
            jax.ShapeDtypeStruct((t, 1), f32),
            jax.ShapeDtypeStruct((block, r), bf16),
        ),
        compiler_params=params,
        name="prepare",
    )(jnp.stack([me, spot]).astype(jnp.int32), tokens, cotangent, down_weight, norm_gain)
    downs = gather_section(weight)
    token_rows = lax.all_to_all(token_send, "dp", 0, 0, tiled=True)

    pairs = gram_pairs(count)
    left = lax.dynamic_slice_in_dim(jnp.array([a for a, _ in pairs], jnp.int32), me * (count - 1), count - 1)
    codes = jnp.array([b % 2 if b < count else 2 + b - count for _, b in pairs], jnp.int32)
    right = lax.dynamic_slice_in_dim(codes, me * (count - 1), count - 1)
    gram = pl.pallas_call(
        functools.partial(gram_kernel, count),
        out_shape=jax.ShapeDtypeStruct((count - 1, r, r), bf16),
        in_specs=[smem] * 3 + [vmem] * (count + 2),
        out_specs=vmem,
        scratch_shapes=[pltpu.VMEM((2 + count, block, r), bf16)],
        compiler_params=params,
        name="gram",
    )(order, left, right, *ups, downs[0], downs[count // 2])
    line = jnp.zeros((peers, 16, r), bf16).at[:, 0, : lengths.shape[1]].set(lengths.astype(bf16))
    gram_rows = (count - 1) * r // peers
    cot_rows = cot_send.shape[1]
    packed = jnp.concatenate([cot_send, gram.reshape(peers, gram_rows, r), line], axis=1)
    packed, token_rows = lax.optimization_barrier((packed, token_rows))
    packed = lax.all_to_all(packed, "dp", 0, 0, tiled=True)

    room = -(-gram_rows // t) * t
    part = pl.pallas_call(
        functools.partial(project_kernel, count, room),
        out_shape=jax.ShapeDtypeStruct((peers, room + (2 * count - 1) * t, r), bf16),
        in_specs=[smem] + [vmem] * (1 + 2 * count),
        out_specs=vmem,
        compiler_params=params,
        name="project",
    )(order, token_rows, *downs, *ups)
    gram_sum = jnp.sum(packed[:, cot_rows : cot_rows + gram_rows].astype(f32), axis=0).astype(bf16)
    all_lengths = packed[:, cot_rows + gram_rows, : lengths.shape[1]].astype(jnp.int32)
    part = part.at[:, :gram_rows].set(jnp.broadcast_to(gram_sum[None], (peers,) + gram_sum.shape))
    sums = lax.all_to_all(part, "dp", 0, 0, tiled=True)

    back_part = pl.pallas_call(
        functools.partial(project_cot_kernel, count),
        out_shape=jax.ShapeDtypeStruct((peers, count * t, r), bf16),
        in_specs=[smem] + [vmem] * (1 + count),
        out_specs=vmem,
        compiler_params=params,
        name="project_cot",
    )(order, packed, *ups)
    all_rows = gather_section(token_rows)
    sums, all_rows = lax.optimization_barrier((sums, all_rows))
    back_sums = lax.all_to_all(back_part, "dp", 0, 0, tiled=True)
    grams = gather_section(sums[:, :gram_rows].reshape(count - 1, r, r))

    held = pl.pallas_call(
        functools.partial(recur_kernel, count, width, room),
        out_shape=jax.ShapeDtypeStruct((count // 2, count + 1, t, r), bf16),
        in_specs=[smem] + [vmem] * (3 + count),
        out_specs=vmem,
        scratch_shapes=[
            pltpu.VMEM((count * (count - 1), r, r), bf16),
            pltpu.VMEM((count, t, r), bf16),
        ],
        compiler_params=params,
        name="recur",
    )(order, sums, back_sums, square, *grams)
    same = spread(jnp.stack([held[0]] + [chip_shift(held[j], j) for j in range(1, count // 2)]))
    other = core_swap(same)

    ends = jnp.cumsum(all_lengths, axis=1)
    position = (order[:, None] * t + jnp.arange(t, dtype=jnp.int32)[None]).reshape(-1)
    seg = jnp.sum(position[None, None, :] >= ends[:, :, None], axis=1).astype(jnp.int32)
    seg = seg.reshape(peers, 1, row_count)
    gain = lax.dynamic_slice_in_dim(norm_gain, spot * block, block, 1)

    seqs = lengths.shape[1]
    chunk = min(r, block)
    fisher = pl.pallas_call(
        functools.partial(fisher_kernel, count, seqs, 1.0 / (row_count * peers)),
        out_shape=jax.ShapeDtypeStruct((block, r), f32),
        in_specs=[smem, smem] + [vmem] * (2 * count + 4),
        out_specs=vmem,
        scratch_shapes=[
            pltpu.VMEM((r, chunk), f32),
            pltpu.VMEM((peers, row_count, chunk), bf16),
            pltpu.VMEM((peers, seqs * r, row_count), bf16),
        ],
        compiler_params=params,
        name="squares",
    )(order, me.astype(jnp.int32)[None], *all_rows, *ups, same, other, seg, gain)
    return fisher[None]


def solution(mesh):
    in_specs = (
        P("dp", None),
        P("dp", None),
        P("section", "dp", None),
        P("section", "dp", None),
        P("section", None),
        P("dp", None),
    )
    out_specs = P("section", "dp", None)
    return jax.shard_map(
        per_device, mesh=mesh, in_specs=in_specs, out_specs=out_specs, check_vma=False
    )
```

```python
import functools

import jax
import jax.numpy as jnp
from jax import lax
from jax.experimental import pallas as pl
from jax.experimental.pallas import tpu as pltpu
from jax.sharding import PartitionSpec as P

epsilon = 1e-05
bf16 = jnp.bfloat16
f32 = jnp.float32
VMEM_BYTES = 56 * 1024 * 1024


def dot(a, b, ca, cb):
    return lax.dot_general(a, b, (((ca,), (cb,)), ((), ())), preferred_element_type=f32)


def core_swap(x):
    count = lax.axis_size("section")
    return lax.ppermute(x, "section", [(i, i ^ 1) for i in range(count)])


def chip_shift(x, by):
    count = lax.axis_size("section")
    return lax.ppermute(x, "section", [(i, (i - 2 * by) % count) for i in range(count)])


def section_order():
    count = lax.axis_size("section")
    me = lax.axis_index("section")
    same = [(me + 2 * j) % count for j in range(count // 2)]
    other = [((me ^ 1) + 2 * j) % count for j in range(count // 2)]
    return jnp.stack(same + other).astype(jnp.int32)


def gather_section(x):
    count = lax.axis_size("section")
    same = [x] + [chip_shift(x, j) for j in range(1, count // 2)]
    return same + [core_swap(b) for b in same]


def pair_swap(x):
    peers = lax.axis_size("dp")
    return lax.ppermute(x, "dp", [(i, i ^ 1) for i in range(peers)])


def line_exchange(x):
    peers = lax.axis_size("dp")
    groups = [list(range(p, peers, 2)) for p in range(2)]
    return lax.all_to_all(x, "dp", 0, 0, axis_index_groups=groups, tiled=True)


def repeated(x, times):
    return jnp.broadcast_to(x[None], (times,) + x.shape)


def gram_pairs(count):
    ups = [(k, count + j) for j in range(count - 1) for k in range(j + 1)]
    listed = []
    for chip in range(count // 2):
        own = [(k, l) for l in (2 * chip, 2 * chip + 1) for k in range(l)]
        spare = 2 * (count - 1) - len(own)
        listed += own + ups[:spare]
        ups = ups[spare:]
    return listed


def prepare_kernel(place, tokens_ref, cot_ref, down_ref, gain_ref, rows_ref, square_ref, weight_ref):
    peers, rows, block = rows_ref.shape
    t = rows // 2
    total = jnp.zeros((t, 1), f32)
    for n in range(peers):
        piece = tokens_ref[:, n * block : (n + 1) * block]
        wide = piece.astype(f32)
        total = total + jnp.sum(wide * wide, axis=-1, keepdims=True)
        rows_ref[n, :t] = piece
        rows_ref[n, t:] = cot_ref[:, n * block : (n + 1) * block]
    square_ref[...] = total
    gain = gain_ref[...].reshape(block, 1)
    weight_ref[...] = (down_ref[0].astype(f32) * gain).astype(bf16)


def gram_kernel(count, order, left, right, *refs):
    ups = refs[:count]
    mine, partner, gram_ref, table = refs[count:]
    core = lax.rem(order[0], 2)
    table[core] = mine[...]
    table[1 - core] = partner[...]
    for i in range(count):
        table[2 + order[i]] = ups[i][...]
    for p in range(count - 1):
        gram_ref[p] = dot(table[2 + left[p]], table[right[p]], 0, 0).astype(bf16)


def project_kernel(count, order, spot, rows_ref, *refs):
    downs = refs[:count]
    ups = refs[count : 2 * count]
    keep_ref, send_ref, tokens_ref = refs[2 * count :]
    peers, rows, width = rows_ref.shape
    t = rows // 2
    half, _, r = keep_ref.shape
    mine = lax.rem(spot[0], 2)
    tokens_ref[...] = rows_ref[:, :t]
    picked = [rows_ref[2 * z + mine, :t] for z in range(half)]
    picked += [rows_ref[2 * z + 1 - mine, :t] for z in range(half)]
    x = jnp.concatenate(picked, axis=0)

    def store(m, out):
        place = pl.ds(pl.multiple_of(m * t, t), t)
        keep_ref[:, place, :] = out[: half * t].reshape(half, t, r)
        send_ref[:, place, :] = out[half * t :].astype(bf16).reshape(half, t, r)

    for i in range(count):
        layer = order[i]
        store(layer, dot(x, downs[i][...], 1, 0))

        @pl.when(layer < count - 1)
        def _():
            store(count + layer, dot(x, ups[i][...], 1, 0))


def project_cot_kernel(count, room, order, rows_ref, *refs):
    ups = refs[:count]
    part_ref = refs[count]
    peers, rows, width = rows_ref.shape
    t = rows // 2
    r = part_ref.shape[2]
    c = rows_ref[:, t:].reshape(peers * t, width)
    for i in range(count):
        out = dot(c, ups[i][...], 1, 0)
        start = pl.multiple_of(room + order[i] * t, t)
        part_ref[:, pl.ds(start, t), :] = out.astype(bf16).reshape(peers, t, r)


def recur_kernel(count, width, room, order, sums_ref, back_ref, sq_ref, *refs):
    grams = refs[:count]
    out_ref, table, grads = refs[count:]
    half, _, t, _ = out_ref.shape
    per = count - 1
    for i in range(count):
        for p in range(per):
            table[order[i] * per + p] = grams[i][p]
    place = {pair: n for n, pair in enumerate(gram_pairs(count))}

    def mixed(k, l):
        return table[place[(k, l)]]

    def ups(k, j, a):
        if k <= j:
            return dot(a, table[place[(k, count + j)]], 1, 0)
        return dot(a, table[place[(j, count + k)]], 1, 1)

    def total(ref, start):
        return jnp.sum(ref[:, start : start + t].astype(f32), axis=0)

    proj = [total(sums_ref, l * t) for l in range(count)]
    hu = [total(sums_ref, (count + k) * t) for k in range(count - 1)]
    back = [total(back_ref, room + l * t) for l in range(count)]
    norm = sq_ref[...]
    invs, pres, hus = [], [], []
    for l in range(count):
        inv = lax.rsqrt(norm / width + epsilon)
        pre = inv * proj[l]
        invs.append(inv)
        pres.append(pre)
        hus.append(list(hu))
        if l < count - 1:
            act = (pre * jax.nn.sigmoid(pre)).astype(bf16)
            for j in range(half):
                out_ref[j, 2 + l] = act
            wide = act.astype(f32)
            for j in range(l + 1, count):
                proj[j] = proj[j] + dot(act, mixed(l, j), 1, 0)
            step = [ups(l, j, act) for j in range(count - 1)]
            norm = norm + jnp.sum(wide * (2.0 * hu[l] + step[l]), axis=-1, keepdims=True)
            hu = [hu[j] + step[j] for j in range(count - 1)]
    for l in reversed(range(count)):
        s = jax.nn.sigmoid(pres[l])
        grad = (back[l] * s * (1.0 + pres[l] * (1.0 - s))).astype(bf16)
        wide = grad.astype(f32)
        grads[l] = (wide * invs[l]).astype(bf16)
        inner = jnp.sum(wide * proj[l], axis=-1, keepdims=True) / width
        for j in range(l):
            back[j] = back[j] + invs[l] * (
                dot(grad, mixed(j, l), 1, 1) - invs[l] * invs[l] * inner * hus[l][j]
            )
    chip = order[0] // 2
    for j in range(half):
        other = lax.rem(chip + half - j, half)
        out_ref[j, 0] = grads[2 * other]
        out_ref[j, 1] = grads[2 * other + 1]


def fisher_kernel(count, seqs, scale, order, place, *refs):
    half = count // 2
    rows = refs[:count]
    ups = refs[count : 2 * count]
    states = refs[2 * count : 4 * count]
    seg_ref, gain_ref, out_ref, acc, hidden, masks = refs[4 * count :]
    peers, t, width = rows[0].shape
    r = out_ref.shape[1]
    chunk = min(r, width)
    span = count * t
    me = place[0]
    mine = lax.rem(place[1], 2)
    line = peers // 2
    names = [2 * (n % line) + (mine if n < line else 1 - mine) for n in range(peers)]

    def column(n, m):
        first = n // line * count
        return jnp.concatenate([states[first + i][n % line, m] for i in range(count)], axis=0)

    acts = []
    for i in range(1, count):
        act = jnp.concatenate([column(n, 2 + jnp.minimum(order[i], count - 2)) for n in range(peers)], axis=0)
        acts.append(jnp.where(order[i] < me, act, jnp.zeros_like(act)))
    for n in range(peers):
        grad = column(n, lax.rem(me, 2)).astype(f32).T
        seg = seg_ref[names[n]]
        for q in range(seqs):
            masks[n, q * r : (q + 1) * r] = jnp.where(seg == q, grad, 0.0).astype(bf16)
    for f in range(width // chunk):
        cols = slice(f * chunk, (f + 1) * chunk)
        update = dot(acts[0], ups[1][cols], 1, 1)
        for i in range(2, count):
            update = update + dot(acts[i - 1], ups[i][cols], 1, 1)
        for n in range(peers):
            h = jnp.concatenate([rows[i][names[n], :, cols] for i in range(count)], axis=0).astype(f32)
            hidden[n] = (h + update[n * span : (n + 1) * span]).astype(bf16)
        for n in range(peers):
            g = dot(masks[n], hidden[n], 1, 0)
            g = g * g
            total = g[:r]
            for q in range(1, seqs):
                total = total + g[q * r : (q + 1) * r]
            if n == 0:
                acc[...] = total
            else:
                acc[...] = acc[...] + total
        gain = gain_ref[:, cols]
        out_ref[cols] = (acc[...] * (gain * gain * scale)).T


def per_device(tokens, cotangent, down_weight, up_weight, norm_gain, lengths):
    count = lax.axis_size("section")
    peers = lax.axis_size("dp")
    me = lax.axis_index("section")
    spot = lax.axis_index("dp")
    row_count, width = tokens.shape
    block = width // peers
    t = row_count // count
    r = down_weight.shape[2]
    order = section_order()
    params = pltpu.CompilerParams(vmem_limit_bytes=VMEM_BYTES)
    smem = pl.BlockSpec(memory_space=pltpu.SMEM)
    vmem = pl.BlockSpec(memory_space=pltpu.VMEM)

    ups = gather_section(up_weight[0])
    place = jnp.stack([me, spot]).astype(jnp.int32)
    send, square, weight = pl.pallas_call(
        prepare_kernel,
        grid_spec=pltpu.PrefetchScalarGridSpec(
            num_scalar_prefetch=1,
            grid=(1,),
            in_specs=[
                pl.BlockSpec((t, width), lambda n, place: (place[0], 0)),
                pl.BlockSpec((t, width), lambda n, place: (place[0], 0)),
                pl.BlockSpec((1, block, r), lambda n, place: (0, 0, 0)),
                pl.BlockSpec((1, block), lambda n, place: (0, place[1])),
            ],
            out_specs=[
                pl.BlockSpec((peers, 2 * t, block), lambda n, place: (0, 0, 0)),
                pl.BlockSpec((t, 1), lambda n, place: (0, 0)),
                pl.BlockSpec((block, r), lambda n, place: (0, 0)),
            ],
        ),
        out_shape=(
            jax.ShapeDtypeStruct((peers, 2 * t, block), bf16),
            jax.ShapeDtypeStruct((t, 1), f32),
            jax.ShapeDtypeStruct((block, r), bf16),
        ),
        compiler_params=params,
        name="prepare",
    )(place, tokens, cotangent, down_weight, norm_gain)
    downs = gather_section(weight)
    rows = lax.all_to_all(send, "dp", 0, 0, tiled=True)

    pairs = gram_pairs(count)
    left = lax.dynamic_slice_in_dim(jnp.array([a for a, _ in pairs], jnp.int32), me * (count - 1), count - 1)
    codes = jnp.array([b % 2 if b < count else 2 + b - count for _, b in pairs], jnp.int32)
    right = lax.dynamic_slice_in_dim(codes, me * (count - 1), count - 1)
    gram = pl.pallas_call(
        functools.partial(gram_kernel, count),
        out_shape=jax.ShapeDtypeStruct((count - 1, r, r), bf16),
        in_specs=[smem] * 3 + [vmem] * (count + 2),
        out_specs=vmem,
        scratch_shapes=[pltpu.VMEM((2 + count, block, r), bf16)],
        compiler_params=params,
        name="gram",
    )(order, left, right, *ups, downs[0], downs[count // 2])
    line = jnp.zeros((peers, 16, r), bf16).at[:, 0, : lengths.shape[1]].set(lengths.astype(bf16))
    gram_rows = (count - 1) * r // peers
    packed = jnp.concatenate([gram.reshape(peers, gram_rows, r), line], axis=1)
    packed, rows = lax.optimization_barrier((packed, rows))
    packed = lax.all_to_all(packed, "dp", 0, 0, tiled=True)

    room = -(-gram_rows // t) * t
    back_part = pl.pallas_call(
        functools.partial(project_cot_kernel, count, room),
        out_shape=jax.ShapeDtypeStruct((peers, room + count * t, r), bf16),
        in_specs=[smem] + [vmem] * (1 + count),
        out_specs=vmem,
        compiler_params=params,
        name="project_cot",
    )(order, rows, *ups)
    keep, give, token_rows = pl.pallas_call(
        functools.partial(project_kernel, count),
        out_shape=(
            jax.ShapeDtypeStruct((peers // 2, (2 * count - 1) * t, r), f32),
            jax.ShapeDtypeStruct((peers // 2, (2 * count - 1) * t, r), bf16),
            jax.ShapeDtypeStruct((peers, t, block), bf16),
        ),
        in_specs=[smem, smem] + [vmem] * (1 + 2 * count),
        out_specs=(vmem, vmem, vmem),
        compiler_params=params,
        name="project",
    )(order, spot.astype(jnp.int32)[None], rows, *downs, *ups)
    part = (keep + pair_swap(give).astype(f32)).astype(bf16)
    gram_sum = jnp.sum(packed[:, :gram_rows].astype(f32), axis=0).astype(bf16)
    all_lengths = packed[:, gram_rows, : lengths.shape[1]].astype(jnp.int32)
    back_part = back_part.at[:, :gram_rows].set(repeated(gram_sum, peers))
    back_sums = lax.all_to_all(back_part, "dp", 0, 0, tiled=True)
    all_rows = gather_section(token_rows)
    back_sums, part, all_rows = lax.optimization_barrier((back_sums, part, all_rows))
    sums = line_exchange(part)
    grams = gather_section(back_sums[:, :gram_rows].reshape(count - 1, r, r))

    held = pl.pallas_call(
        functools.partial(recur_kernel, count, width, room),
        out_shape=jax.ShapeDtypeStruct((count // 2, count + 1, t, r), bf16),
        in_specs=[smem] + [vmem] * (3 + count),
        out_specs=vmem,
        scratch_shapes=[
            pltpu.VMEM((count * (count - 1), r, r), bf16),
            pltpu.VMEM((count, t, r), bf16),
        ],
        compiler_params=params,
        name="recur",
    )(order, sums, back_sums, square, *grams)
    ends = jnp.cumsum(all_lengths, axis=1)
    position = (order[:, None] * t + jnp.arange(t, dtype=jnp.int32)[None]).reshape(-1)
    seg = jnp.sum(position[None, None, :] >= ends[:, :, None], axis=1).astype(jnp.int32)
    seg = seg.reshape(peers, 1, row_count)
    gain = lax.dynamic_slice_in_dim(norm_gain, spot * block, block, 1)
    held, seg, gain = lax.optimization_barrier((held, seg, gain))

    line = peers // 2
    states = [[None] * count, [None] * count]
    for j in range(count // 2):
        block_j = chip_shift(held[j], j) if j else held[0]
        got = line_exchange(repeated(block_j, line))
        for p, part in enumerate((got, pair_swap(got))):
            states[p][j] = part
            states[p][count // 2 + j] = core_swap(part)

    seqs = lengths.shape[1]
    chunk = min(r, block)
    fisher = pl.pallas_call(
        functools.partial(fisher_kernel, count, seqs, 1.0 / (row_count * peers)),
        out_shape=jax.ShapeDtypeStruct((block, r), f32),
        in_specs=[smem, smem] + [vmem] * (4 * count + 2),
        out_specs=vmem,
        scratch_shapes=[
            pltpu.VMEM((r, chunk), f32),
            pltpu.VMEM((peers, row_count, chunk), bf16),
            pltpu.VMEM((peers, seqs * r, row_count), bf16),
        ],
        compiler_params=params,
        name="squares",
    )(order, place, *all_rows, *ups, *states[0], *states[1], seg, gain)
    return fisher[None]


def solution(mesh):
    in_specs = (
        P("dp", None),
        P("dp", None),
        P("section", "dp", None),
        P("section", "dp", None),
        P("section", None),
        P("dp", None),
    )
    out_specs = P("section", "dp", None)
    return jax.shard_map(
        per_device, mesh=mesh, in_specs=in_specs, out_specs=out_specs, check_vma=False
    )
```

```python
import functools

import jax
import jax.numpy as jnp
from jax import lax
from jax.experimental import pallas as pl
from jax.experimental.pallas import tpu as pltpu
from jax.sharding import PartitionSpec as P

epsilon = 1e-05
bf16 = jnp.bfloat16
f32 = jnp.float32
MIB = 1024 * 1024


def dot(a, b, ca, cb):
    return lax.dot_general(a, b, (((ca,), (cb,)), ((), ())), preferred_element_type=f32)


def core_swap(x):
    count = lax.axis_size("section")
    return lax.ppermute(x, "section", [(i, i ^ 1) for i in range(count)])


def chip_shift(x, by):
    count = lax.axis_size("section")
    return lax.ppermute(x, "section", [(i, (i - 2 * by) % count) for i in range(count)])


def section_order():
    count = lax.axis_size("section")
    me = lax.axis_index("section")
    same = [(me + 2 * j) % count for j in range(count // 2)]
    other = [((me ^ 1) + 2 * j) % count for j in range(count // 2)]
    return jnp.stack(same + other).astype(jnp.int32)


def gather_section(x):
    count = lax.axis_size("section")
    same = [x] + [chip_shift(x, j) for j in range(1, count // 2)]
    return same + [core_swap(b) for b in same]


def far_away(*arrays):
    return [pltpu.with_memory_space_constraint(a, pltpu.HBM) for a in arrays]


def pair_swap(x):
    peers = lax.axis_size("dp")
    return lax.ppermute(x, "dp", [(i, i ^ 1) for i in range(peers)])


def line_exchange(x):
    peers = lax.axis_size("dp")
    groups = [list(range(p, peers, 2)) for p in range(2)]
    return lax.all_to_all(x, "dp", 0, 0, axis_index_groups=groups, tiled=True)


def repeated(x, times):
    return jnp.broadcast_to(x[None], (times,) + x.shape)


def gram_pairs(count):
    ups = [(k, count + j) for j in range(count - 1) for k in range(j + 1)]
    listed = []
    for chip in range(count // 2):
        own = [(k, l) for l in (2 * chip, 2 * chip + 1) for k in range(l)]
        spare = 2 * (count - 1) - len(own)
        listed += own + ups[:spare]
        ups = ups[spare:]
    return listed


def prepare_kernel(tokens_ref, cot_ref, rows_ref, sems):
    peers, rows, block = rows_ref.shape
    t = rows // 2
    start = pl.multiple_of(lax.axis_index("section") * t, t)
    copies = []
    for n in range(peers):
        for k, ref in enumerate((tokens_ref, cot_ref)):
            source = ref.at[pl.ds(start, t), pl.ds(n * block, block)]
            copies.append(pltpu.make_async_copy(source, rows_ref.at[n, pl.ds(k * t, t)], sems.at[k, n]))
    for copy in copies:
        copy.start()
    for copy in copies:
        copy.wait()


def weight_kernel(place, rows_ref, down_ref, gain_ref, square_ref, weight_ref):
    peers, rows, block = rows_ref.shape
    t = rows // 2
    total = jnp.zeros((t, 1), f32)
    for n in range(peers):
        wide = rows_ref[n, :t].astype(f32)
        total = total + jnp.sum(wide * wide, axis=-1, keepdims=True)
    square_ref[...] = total
    gain = gain_ref[...].reshape(block, 1)
    weight_ref[...] = (down_ref[0].astype(f32) * gain).astype(bf16)


def gram_kernel(count, seqs, order, left, right, lengths, *refs):
    ups = refs[:count]
    mine, partner, gram_ref, table = refs[count:]
    peers, rows, r = gram_ref.shape
    core = lax.rem(order[0], 2)
    table[core] = mine[...]
    table[1 - core] = partner[...]
    for i in range(count):
        table[2 + order[i]] = ups[i][...]
    share = r // peers
    for p in range(count - 1):
        out = dot(table[2 + left[p]], table[right[p]], 0, 0).astype(bf16)
        gram_ref[:, p * share : (p + 1) * share] = out.reshape(peers, share, r)
    used = (count - 1) * share
    lane = lax.broadcasted_iota(jnp.int32, (rows - used, r), 1)
    line = jnp.zeros((rows - used, r), f32)
    for q in range(seqs):
        line = jnp.where(lane == q, lengths[0, q].astype(f32), line)
    gram_ref[:, used:] = jnp.broadcast_to(line.astype(bf16)[None], (peers, rows - used, r))


def paired(rows, mine):
    return jnp.concatenate(rows(mine) + rows(1 - mine), axis=0)


def store_pair(keep_ref, send_ref, m, t, out):
    line, _, r = keep_ref.shape
    place = pl.ds(pl.multiple_of(m * t, t), t)
    keep_ref[:, place, :] = out[: line * t].reshape(line, t, r)
    send_ref[:, place, :] = out[line * t :].astype(bf16).reshape(line, t, r)


def project_kernel(count, order, spot, rows_ref, *refs):
    downs = refs[:count]
    ups = refs[count : 2 * count]
    keep_ref, send_ref, tokens_ref = refs[2 * count :]
    peers, rows, _ = rows_ref.shape
    t = rows // 2
    mine = lax.rem(spot[0], 2)
    tokens_ref[...] = rows_ref[:, :t]
    x = paired(lambda p: [rows_ref[2 * z + p, :t] for z in range(peers // 2)], mine)
    c = paired(lambda p: [rows_ref[2 * z + p, t:] for z in range(peers // 2)], mine)
    for i in range(count):
        layer = order[i]
        store_pair(keep_ref, send_ref, layer, t, dot(x, downs[i][...], 1, 0))
        store_pair(keep_ref, send_ref, 2 * count - 1 + layer, t, dot(c, ups[i][...], 1, 0))

        @pl.when(layer < count - 1)
        def _():
            store_pair(keep_ref, send_ref, count + layer, t, dot(x, ups[i][...], 1, 0))


def recur_kernel(count, width, order, spot, sums_ref, sq_ref, *refs):
    grams = refs[: 2 * count]
    own_ref, out_ref, table, grads = refs[2 * count :]
    copies, _, t, _ = own_ref.shape
    half = count // 2

    def put(j, m, value):
        if j:
            out_ref[j - 1, m] = value
        else:
            for z in range(copies):
                own_ref[z, m] = value

    per = count - 1
    mine = lax.rem(spot[0], 2)
    line = grams[0].shape[0]
    _, _, peers, share, r = table.shape
    for i in range(count):
        for z in range(line):
            for p in range(per):
                rows = slice(p * share, (p + 1) * share)
                table[order[i], p, 2 * z + mine] = grams[i][z, rows]
                table[order[i], p, 2 * z + 1 - mine] = grams[count + i][z, rows]
    place = {pair: n for n, pair in enumerate(gram_pairs(count))}

    def product(pair):
        n = place[pair]
        return table[n // per, n % per].reshape(peers * share, r)

    def mixed(k, l):
        return product((k, l))

    def ups(k, j, a):
        if k <= j:
            return dot(a, product((k, count + j)), 1, 0)
        return dot(a, product((j, count + k)), 1, 1)

    def total(ref, start):
        return jnp.sum(ref[:, start : start + t].astype(f32), axis=0)

    proj = [total(sums_ref, l * t) for l in range(count)]
    hu = [total(sums_ref, (count + k) * t) for k in range(count - 1)]
    back = [total(sums_ref, (2 * count - 1 + l) * t) for l in range(count)]
    norm = sq_ref[...]
    invs, pres, hus = [], [], []
    for l in range(count):
        inv = lax.rsqrt(norm / width + epsilon)
        pre = inv * proj[l]
        invs.append(inv)
        pres.append(pre)
        hus.append(list(hu))
        if l < count - 1:
            act = (pre * jax.nn.sigmoid(pre)).astype(bf16)
            for j in range(half):
                put(j, 2 + l, act)
            wide = act.astype(f32)
            for j in range(l + 1, count):
                proj[j] = proj[j] + dot(act, mixed(l, j), 1, 0)
            step = [ups(l, j, act) for j in range(count - 1)]
            norm = norm + jnp.sum(wide * (2.0 * hu[l] + step[l]), axis=-1, keepdims=True)
            hu = [hu[j] + step[j] for j in range(count - 1)]
    for l in reversed(range(count)):
        s = jax.nn.sigmoid(pres[l])
        grad = (back[l] * s * (1.0 + pres[l] * (1.0 - s))).astype(bf16)
        wide = grad.astype(f32)
        grads[l] = (wide * invs[l]).astype(bf16)
        inner = jnp.sum(wide * proj[l], axis=-1, keepdims=True) / width
        for j in range(l):
            back[j] = back[j] + invs[l] * (
                dot(grad, mixed(j, l), 1, 1) - invs[l] * invs[l] * inner * hus[l][j]
            )
    chip = order[0] // 2
    for j in range(half):
        other = lax.rem(chip + half - j, half)
        put(j, 0, grads[2 * other])
        put(j, 1, grads[2 * other + 1])


def fisher_kernel(count, seqs, scale, order, place, lengths, *refs):
    half = count // 2
    sources = refs[:count]
    ups = refs[count : 2 * count]
    states = refs[2 * count : 4 * count]
    gain_ref, out_ref, rows, acc, hidden, masks, sems = refs[4 * count :]
    copies = [pltpu.make_async_copy(sources[i], rows.at[i], sems.at[i]) for i in range(count)]
    for copy in copies:
        copy.start()
    _, peers, t, width = rows.shape
    r = out_ref.shape[1]
    chunk = min(r, width)
    span = count * t
    me = place[0]
    mine = lax.rem(place[1], 2)
    line = peers // 2
    names = [2 * (n % line) + (mine if n < line else 1 - mine) for n in range(peers)]
    spot = lax.broadcasted_iota(jnp.int32, (1, span), 1)
    position = spot
    for i in range(count):
        inside = (spot >= i * t) & (spot < (i + 1) * t)
        position = jnp.where(inside, spot + (order[i] - i) * t, position)

    def column(n, m):
        first = n // line * count
        return jnp.concatenate([states[first + i][n % line, m] for i in range(count)], axis=0)

    acts = []
    for i in range(1, count):
        act = jnp.concatenate([column(n, 2 + jnp.minimum(order[i], count - 2)) for n in range(peers)], axis=0)
        acts.append(jnp.where(order[i] < me, act, jnp.zeros_like(act)))
    for n in range(peers):
        grad = column(n, lax.rem(me, 2)).astype(f32).T
        start = 0
        for q in range(seqs):
            stop = start + lengths[names[n], q]
            inside = (position >= start) & (position < stop)
            masks[n, q * r : (q + 1) * r] = jnp.where(inside, grad, 0.0).astype(bf16)
            start = stop
    for f in range(width // chunk):
        cols = slice(f * chunk, (f + 1) * chunk)
        update = dot(acts[0], ups[1][cols], 1, 1)
        for i in range(2, count):
            update = update + dot(acts[i - 1], ups[i][cols], 1, 1)
        if f == 0:
            for copy in copies:
                copy.wait()
        for n in range(peers):
            h = jnp.concatenate([rows[i, names[n], :, cols] for i in range(count)], axis=0).astype(f32)
            hidden[n] = (h + update[n * span : (n + 1) * span]).astype(bf16)
        for n in range(peers):
            g = dot(masks[n], hidden[n], 1, 0)
            g = g * g
            total = g[:r]
            for q in range(1, seqs):
                total = total + g[q * r : (q + 1) * r]
            if n == 0:
                acc[...] = total
            else:
                acc[...] = acc[...] + total
        gain = gain_ref[:, cols]
        out_ref[cols] = (acc[...] * (gain * gain * scale)).T


def per_device(tokens, cotangent, down_weight, up_weight, norm_gain, lengths):
    count = lax.axis_size("section")
    peers = lax.axis_size("dp")
    me = lax.axis_index("section")
    spot = lax.axis_index("dp")
    row_count, width = tokens.shape
    block = width // peers
    t = row_count // count
    r = down_weight.shape[2]
    order = section_order()
    smem = pl.BlockSpec(memory_space=pltpu.SMEM)
    vmem = pl.BlockSpec(memory_space=pltpu.VMEM)
    anywhere = pl.BlockSpec(memory_space=pl.ANY)

    def limit(mib):
        return pltpu.CompilerParams(vmem_limit_bytes=mib * MIB)

    place = jnp.stack([me, spot]).astype(jnp.int32)
    spot_ref = place[1:]
    ups = gather_section(up_weight[0])
    send = pl.pallas_call(
        prepare_kernel,
        out_shape=jax.ShapeDtypeStruct((peers, 2 * t, block), bf16),
        in_specs=[anywhere, anywhere],
        out_specs=vmem,
        scratch_shapes=[pltpu.SemaphoreType.DMA((2, peers))],
        name="prepare",
    )(tokens, cotangent)
    square, weight = pl.pallas_call(
        weight_kernel,
        grid_spec=pltpu.PrefetchScalarGridSpec(
            num_scalar_prefetch=1,
            grid=(1,),
            in_specs=[
                pl.BlockSpec((peers, 2 * t, block), lambda n, place: (0, 0, 0)),
                pl.BlockSpec((1, block, r), lambda n, place: (0, 0, 0)),
                pl.BlockSpec((1, block), lambda n, place: (0, place[1])),
            ],
            out_specs=[
                pl.BlockSpec((t, 1), lambda n, place: (0, 0)),
                pl.BlockSpec((block, r), lambda n, place: (0, 0)),
            ],
        ),
        out_shape=(
            jax.ShapeDtypeStruct((t, 1), f32),
            jax.ShapeDtypeStruct((block, r), bf16),
        ),
        compiler_params=limit(12),
        name="weight",
    )(place, send, down_weight, norm_gain)
    partner = core_swap(weight)
    rows = lax.all_to_all(send, "dp", 0, 0, tiled=True)

    pairs = gram_pairs(count)
    left = lax.dynamic_slice_in_dim(jnp.array([a for a, _ in pairs], jnp.int32), me * (count - 1), count - 1)
    codes = jnp.array([b % 2 if b < count else 2 + b - count for _, b in pairs], jnp.int32)
    right = lax.dynamic_slice_in_dim(codes, me * (count - 1), count - 1)
    seqs = lengths.shape[1]
    gram_rows = (count - 1) * (r // peers)
    packed = pl.pallas_call(
        functools.partial(gram_kernel, count, seqs),
        out_shape=jax.ShapeDtypeStruct((peers, gram_rows + 16, r), bf16),
        in_specs=[smem] * 4 + [vmem] * (count + 2),
        out_specs=vmem,
        scratch_shapes=[pltpu.VMEM((2 + count, block, r), bf16)],
        compiler_params=limit(16),
        name="gram",
    )(order, left, right, lengths, *ups, weight, partner)
    packed, weight = lax.optimization_barrier((packed, weight))
    far = [chip_shift(weight, j) for j in range(1, count // 2)]
    downs = [weight, *far, partner, *[core_swap(b) for b in far]]

    packed = lax.all_to_all(packed, "dp", 0, 0, tiled=True)

    line = peers // 2
    sums_shape = (line, (3 * count - 1) * t, r)
    keep, give, token_rows = pl.pallas_call(
        functools.partial(project_kernel, count),
        out_shape=(
            jax.ShapeDtypeStruct(sums_shape, f32),
            jax.ShapeDtypeStruct(sums_shape, bf16),
            jax.ShapeDtypeStruct((peers, t, block), bf16),
        ),
        in_specs=[smem, smem] + [vmem] * (1 + 2 * count),
        out_specs=(vmem, vmem, vmem),
        compiler_params=limit(16),
        name="project",
    )(order, spot_ref, rows, *downs, *ups)
    gram_sum = jnp.sum(packed[:, :gram_rows].astype(f32), axis=0).astype(bf16)
    all_lengths = packed[:, gram_rows, :seqs].astype(jnp.int32)
    own_grams = line_exchange(repeated(gram_sum, line))
    part = (keep + pair_swap(give).astype(f32)).astype(bf16)
    far_rows = [chip_shift(token_rows, j) for j in range(1, count // 2)]
    own_grams, part, *far_rows = lax.optimization_barrier((own_grams, part, *far_rows))
    sums = line_exchange(part)
    all_rows = [token_rows, *far_rows]
    all_rows += [core_swap(b) for b in all_rows]
    sums, all_rows = lax.optimization_barrier((sums, all_rows))
    grams = gather_section(own_grams) + gather_section(pair_swap(own_grams))

    own_held, held = pl.pallas_call(
        functools.partial(recur_kernel, count, width),
        out_shape=(
            jax.ShapeDtypeStruct((line, count + 1, t, r), bf16),
            jax.ShapeDtypeStruct((count // 2 - 1, count + 1, t, r), bf16),
        ),
        in_specs=[smem, smem] + [vmem] * (2 + 2 * count),
        out_specs=(vmem, vmem),
        scratch_shapes=[
            pltpu.VMEM((count, count - 1, peers, r // peers, r), bf16),
            pltpu.VMEM((count, t, r), bf16),
        ],
        compiler_params=limit(16),
        name="recur",
    )(order, spot_ref, sums, square, *grams)
    gain = lax.dynamic_slice_in_dim(norm_gain, spot * block, block, 1)
    own_held, all_lengths, gain = lax.optimization_barrier((own_held, all_lengths, gain))

    states = [[None] * count, [None] * count]
    for j in range(count // 2):
        block_j = repeated(chip_shift(held[j - 1], j), line) if j else own_held
        got = line_exchange(block_j)
        for p, part in enumerate((got, pair_swap(got))):
            states[p][j] = part
            states[p][count // 2 + j] = core_swap(part)

    chunk = min(r, block)
    fisher = pl.pallas_call(
        functools.partial(fisher_kernel, count, seqs, 1.0 / (row_count * peers)),
        out_shape=jax.ShapeDtypeStruct((block, r), f32),
        in_specs=[smem, smem, smem] + [anywhere] * count + [vmem] * (3 * count + 1),
        out_specs=vmem,
        scratch_shapes=[
            pltpu.VMEM((count, peers, t, block), bf16),
            pltpu.VMEM((r, chunk), f32),
            pltpu.VMEM((peers, row_count, chunk), bf16),
            pltpu.VMEM((peers, seqs * r, row_count), bf16),
            pltpu.SemaphoreType.DMA((count,)),
        ],
        compiler_params=limit(24),
        name="squares",
    )(order, place, all_lengths, *far_away(*all_rows), *ups, *states[0], *states[1], gain)
    return fisher[None]


def solution(mesh):
    in_specs = (
        P("dp", None),
        P("dp", None),
        P("section", "dp", None),
        P("section", "dp", None),
        P("section", None),
        P("dp", None),
    )
    out_specs = P("section", "dp", None)
    return jax.shard_map(
        per_device, mesh=mesh, in_specs=in_specs, out_specs=out_specs, check_vma=False
    )
```

```python
import functools

import jax
import jax.numpy as jnp
from jax import lax
from jax.experimental import pallas as pl
from jax.experimental.pallas import tpu as pltpu
from jax.sharding import PartitionSpec as P

epsilon = 1e-05
bf16 = jnp.bfloat16
f32 = jnp.float32
MIB = 1024 * 1024


def dot(a, b, ca, cb):
    return lax.dot_general(a, b, (((ca,), (cb,)), ((), ())), preferred_element_type=f32)


def core_swap(x):
    count = lax.axis_size("section")
    return lax.ppermute(x, "section", [(i, i ^ 1) for i in range(count)])


def chip_shift(x, by):
    count = lax.axis_size("section")
    return lax.ppermute(x, "section", [(i, (i - 2 * by) % count) for i in range(count)])


def section_order():
    count = lax.axis_size("section")
    me = lax.axis_index("section")
    same = [(me + 2 * j) % count for j in range(count // 2)]
    other = [((me ^ 1) + 2 * j) % count for j in range(count // 2)]
    return jnp.stack(same + other).astype(jnp.int32)


def gather_section(x):
    count = lax.axis_size("section")
    same = [x] + [chip_shift(x, j) for j in range(1, count // 2)]
    return same + [core_swap(b) for b in same]


def kept(x, space):
    return pltpu.with_memory_space_constraint(x, space)


def pair_swap(x):
    peers = lax.axis_size("dp")
    return lax.ppermute(x, "dp", [(i, i ^ 1) for i in range(peers)])


def line_exchange(x):
    peers = lax.axis_size("dp")
    groups = [list(range(p, peers, 2)) for p in range(2)]
    return lax.all_to_all(x, "dp", 0, 0, axis_index_groups=groups, tiled=True)


def repeated(x, times):
    return jnp.broadcast_to(x[None], (times,) + x.shape)


def gram_pairs(count):
    ups = [(k, count + j) for j in range(count - 1) for k in range(j + 1)]
    listed = []
    for chip in range(count // 2):
        own = [(k, l) for l in (2 * chip, 2 * chip + 1) for k in range(l)]
        spare = 2 * (count - 1) - len(own)
        listed += own + ups[:spare]
        ups = ups[spare:]
    return listed


def prepare_kernel(tokens_ref, cot_ref, rows_ref, sems):
    peers, rows, block = rows_ref.shape
    t = rows // 2
    start = pl.multiple_of(lax.axis_index("section") * t, t)
    copies = []
    for n in range(peers):
        for k, ref in enumerate((tokens_ref, cot_ref)):
            source = ref.at[pl.ds(start, t), pl.ds(n * block, block)]
            copies.append(pltpu.make_async_copy(source, rows_ref.at[n, pl.ds(k * t, t)], sems.at[k, n]))
    for copy in copies:
        copy.start()
    for copy in copies:
        copy.wait()


def weight_kernel(place, rows_ref, down_ref, gain_ref, square_ref, weight_ref):
    peers, rows, block = rows_ref.shape
    t = rows // 2
    total = jnp.zeros((t, 1), f32)
    for n in range(peers):
        wide = rows_ref[n, :t].astype(f32)
        total = total + jnp.sum(wide * wide, axis=-1, keepdims=True)
    square_ref[...] = total
    gain = gain_ref[...].reshape(block, 1)
    weight_ref[...] = (down_ref[0].astype(f32) * gain).astype(bf16)


def gram_kernel(count, seqs, order, left, right, lengths, *refs):
    ups = refs[:count]
    mine, partner, gram_ref, table = refs[count:]
    peers, rows, r = gram_ref.shape
    core = lax.rem(order[0], 2)
    table[core] = mine[...]
    table[1 - core] = partner[...]
    for i in range(count):
        table[2 + order[i]] = ups[i][...]
    share = r // peers
    for p in range(count - 1):
        out = dot(table[2 + left[p]], table[right[p]], 0, 0).astype(bf16)
        gram_ref[:, p * share : (p + 1) * share] = out.reshape(peers, share, r)
    used = (count - 1) * share
    lane = lax.broadcasted_iota(jnp.int32, (rows - used, r), 1)
    line = jnp.zeros((rows - used, r), f32)
    for q in range(seqs):
        line = jnp.where(lane == q, lengths[0, q].astype(f32), line)
    gram_ref[:, used:] = jnp.broadcast_to(line.astype(bf16)[None], (peers, rows - used, r))


def paired(rows, mine):
    return jnp.concatenate(rows(mine) + rows(1 - mine), axis=0)


def store_pair(keep_ref, send_ref, m, t, out):
    line, _, r = keep_ref.shape
    place = pl.ds(pl.multiple_of(m * t, t), t)
    keep_ref[:, place, :] = out[: line * t].reshape(line, t, r)
    send_ref[:, place, :] = out[line * t :].astype(bf16).reshape(line, t, r)


def project_kernel(count, order, spot, rows_ref, *refs):
    downs = refs[:count]
    ups = refs[count : 2 * count]
    keep_ref, send_ref = refs[2 * count :]
    peers, rows, _ = rows_ref.shape
    t = rows // 2
    x = paired(lambda p: [rows_ref[2 * z + p, :t] for z in range(peers // 2)], lax.rem(spot[0], 2))
    for i in range(count):
        layer = order[i]
        store_pair(keep_ref, send_ref, layer, t, dot(x, downs[i][...], 1, 0))

        @pl.when(layer < count - 1)
        def _():
            store_pair(keep_ref, send_ref, count + layer, t, dot(x, ups[i][...], 1, 0))


def project_cot_kernel(count, order, spot, rows_ref, *refs):
    ups = refs[:count]
    keep_ref, send_ref, tokens_ref = refs[count:]
    peers, rows, _ = rows_ref.shape
    t = rows // 2
    tokens_ref[...] = rows_ref[:, :t]
    c = paired(lambda p: [rows_ref[2 * z + p, t:] for z in range(peers // 2)], lax.rem(spot[0], 2))
    for i in range(count):
        store_pair(keep_ref, send_ref, order[i], t, dot(c, ups[i][...], 1, 0))


def recur_kernel(count, width, order, spot, sums_ref, sq_ref, *refs):
    grams = refs[: 2 * count]
    own_ref, out_ref, table, grads = refs[2 * count :]
    copies, _, t, _ = own_ref.shape
    half = count // 2

    def put(m, value):
        for z in range(copies):
            own_ref[z, m] = value

    per = count - 1
    mine = lax.rem(spot[0], 2)
    line = grams[0].shape[0]
    _, _, peers, share, r = table.shape
    for i in range(count):
        for z in range(line):
            for p in range(per):
                rows = slice(p * share, (p + 1) * share)
                table[order[i], p, 2 * z + mine] = grams[i][z, rows]
                table[order[i], p, 2 * z + 1 - mine] = grams[count + i][z, rows]
    place = {pair: n for n, pair in enumerate(gram_pairs(count))}

    def product(pair):
        n = place[pair]
        return table[n // per, n % per].reshape(peers * share, r)

    def mixed(k, l):
        return product((k, l))

    def ups(k, j, a):
        if k <= j:
            return dot(a, product((k, count + j)), 1, 0)
        return dot(a, product((j, count + k)), 1, 1)

    def total(ref, start):
        return jnp.sum(ref[:, start : start + t].astype(f32), axis=0)

    proj = [total(sums_ref, l * t) for l in range(count)]
    hu = [total(sums_ref, (count + k) * t) for k in range(count - 1)]
    back = [total(sums_ref, (2 * count - 1 + l) * t) for l in range(count)]
    norm = sq_ref[...]
    invs, pres, hus = [], [], []
    for l in range(count):
        inv = lax.rsqrt(norm / width + epsilon)
        pre = inv * proj[l]
        invs.append(inv)
        pres.append(pre)
        hus.append(list(hu))
        if l < count - 1:
            act = (pre * jax.nn.sigmoid(pre)).astype(bf16)
            put(2 + l, act)
            wide = act.astype(f32)
            for j in range(l + 1, count):
                proj[j] = proj[j] + dot(act, mixed(l, j), 1, 0)
            step = [ups(l, j, act) for j in range(count - 1)]
            norm = norm + jnp.sum(wide * (2.0 * hu[l] + step[l]), axis=-1, keepdims=True)
            hu = [hu[j] + step[j] for j in range(count - 1)]
    for l in reversed(range(count)):
        s = jax.nn.sigmoid(pres[l])
        grad = (back[l] * s * (1.0 + pres[l] * (1.0 - s))).astype(bf16)
        wide = grad.astype(f32)
        grads[l] = (wide * invs[l]).astype(bf16)
        inner = jnp.sum(wide * proj[l], axis=-1, keepdims=True) / width
        for j in range(l):
            back[j] = back[j] + invs[l] * (
                dot(grad, mixed(j, l), 1, 1) - invs[l] * invs[l] * inner * hus[l][j]
            )
    chip = order[0] // 2
    for m in range(2):
        put(m, grads[2 * chip + m])
        for j in range(1, half):
            out_ref[j - 1, m] = grads[2 * lax.rem(chip + half - j, half) + m]


def fisher_kernel(count, seqs, scale, order, place, lengths, *refs):
    half = count // 2
    sources = refs[:count]
    ups = refs[count : 2 * count]
    rest = list(refs[2 * count :])
    states = []
    for i in range(2 * count):
        if i % half:
            states.append((rest.pop(0), rest.pop(0), 0))
        else:
            both = rest.pop(0)
            states.append((both, both, 2))
    gain_ref, out_ref, rows, acc, hidden, masks, sems = rest
    copies = [pltpu.make_async_copy(sources[i], rows.at[i], sems.at[i]) for i in range(count)]
    for copy in copies:
        copy.start()
    _, peers, t, width = rows.shape
    r = out_ref.shape[1]
    chunk = min(r, width)
    span = count * t
    me = place[0]
    mine = lax.rem(place[1], 2)
    line = peers // 2
    names = [2 * (n % line) + (mine if n < line else 1 - mine) for n in range(peers)]
    spot = lax.broadcasted_iota(jnp.int32, (1, span), 1)
    position = spot
    for i in range(count):
        inside = (spot >= i * t) & (spot < (i + 1) * t)
        position = jnp.where(inside, spot + (order[i] - i) * t, position)

    def grad_rows(n, m):
        found = states[n // line * count :][:count]
        return jnp.concatenate([grads[n % line, m] for grads, _, _ in found], axis=0)

    def act_rows(n, k):
        found = states[n // line * count :][:count]
        return jnp.concatenate([acts[n % line, shift + k] for _, acts, shift in found], axis=0)

    acts = []
    for i in range(1, count):
        act = jnp.concatenate([act_rows(n, jnp.minimum(order[i], count - 2)) for n in range(peers)], axis=0)
        acts.append(jnp.where(order[i] < me, act, jnp.zeros_like(act)))
    for n in range(peers):
        grad = grad_rows(n, lax.rem(me, 2)).astype(f32).T
        start = 0
        for q in range(seqs):
            stop = start + lengths[names[n], q]
            inside = (position >= start) & (position < stop)
            masks[n, q * r : (q + 1) * r] = jnp.where(inside, grad, 0.0).astype(bf16)
            start = stop
    for f in range(width // chunk):
        cols = slice(f * chunk, (f + 1) * chunk)
        update = dot(acts[0], ups[1][cols], 1, 1)
        for i in range(2, count):
            update = update + dot(acts[i - 1], ups[i][cols], 1, 1)
        if f == 0:
            for copy in copies:
                copy.wait()
        for n in range(peers):
            h = jnp.concatenate([rows[i, names[n], :, cols] for i in range(count)], axis=0).astype(f32)
            hidden[n] = (h + update[n * span : (n + 1) * span]).astype(bf16)
        for n in range(peers):
            total = None
            for q in range(seqs):
                g = dot(masks[n, q * r : (q + 1) * r], hidden[n], 1, 0)
                total = g * g if total is None else total + g * g
            if n == 0:
                acc[...] = total
            else:
                acc[...] = acc[...] + total
        gain = gain_ref[:, cols]
        out_ref[cols] = (acc[...] * (gain * gain * scale)).T


def per_device(tokens, cotangent, down_weight, up_weight, norm_gain, lengths):
    count = lax.axis_size("section")
    peers = lax.axis_size("dp")
    me = lax.axis_index("section")
    spot = lax.axis_index("dp")
    row_count, width = tokens.shape
    block = width // peers
    t = row_count // count
    r = down_weight.shape[2]
    order = section_order()
    smem = pl.BlockSpec(memory_space=pltpu.SMEM)
    vmem = pl.BlockSpec(memory_space=pltpu.VMEM)
    anywhere = pl.BlockSpec(memory_space=pl.ANY)

    def limit(mib):
        return pltpu.CompilerParams(vmem_limit_bytes=mib * MIB)

    place = jnp.stack([me, spot]).astype(jnp.int32)
    spot_ref = place[1:]
    ups = gather_section(up_weight[0])
    send = pl.pallas_call(
        prepare_kernel,
        out_shape=jax.ShapeDtypeStruct((peers, 2 * t, block), bf16),
        in_specs=[anywhere, anywhere],
        out_specs=vmem,
        scratch_shapes=[pltpu.SemaphoreType.DMA((2, peers))],
        name="prepare",
    )(tokens, cotangent)
    square, weight = pl.pallas_call(
        weight_kernel,
        grid_spec=pltpu.PrefetchScalarGridSpec(
            num_scalar_prefetch=1,
            grid=(1,),
            in_specs=[
                pl.BlockSpec((peers, 2 * t, block), lambda n, place: (0, 0, 0)),
                pl.BlockSpec((1, block, r), lambda n, place: (0, 0, 0)),
                pl.BlockSpec((1, block), lambda n, place: (0, place[1])),
            ],
            out_specs=[
                pl.BlockSpec((t, 1), lambda n, place: (0, 0)),
                pl.BlockSpec((block, r), lambda n, place: (0, 0)),
            ],
        ),
        out_shape=(
            jax.ShapeDtypeStruct((t, 1), f32),
            jax.ShapeDtypeStruct((block, r), bf16),
        ),
        compiler_params=limit(12),
        name="weight",
    )(place, send, down_weight, norm_gain)
    partner = core_swap(weight)
    rows = lax.all_to_all(send, "dp", 0, 0, tiled=True)

    pairs = gram_pairs(count)
    left = lax.dynamic_slice_in_dim(jnp.array([a for a, _ in pairs], jnp.int32), me * (count - 1), count - 1)
    codes = jnp.array([b % 2 if b < count else 2 + b - count for _, b in pairs], jnp.int32)
    right = lax.dynamic_slice_in_dim(codes, me * (count - 1), count - 1)
    seqs = lengths.shape[1]
    gram_rows = (count - 1) * (r // peers)
    packed = pl.pallas_call(
        functools.partial(gram_kernel, count, seqs),
        out_shape=jax.ShapeDtypeStruct((peers, gram_rows + 16, r), bf16),
        in_specs=[smem] * 4 + [vmem] * (count + 2),
        out_specs=vmem,
        scratch_shapes=[pltpu.VMEM((2 + count, block, r), bf16)],
        compiler_params=limit(16),
        name="gram",
    )(order, left, right, lengths, *ups, weight, partner)
    packed, weight = lax.optimization_barrier((packed, weight))
    far = [chip_shift(weight, j) for j in range(1, count // 2)]
    downs = [weight, *far, partner, *[core_swap(b) for b in far]]

    packed = lax.all_to_all(packed, "dp", 0, 0, tiled=True)

    line = peers // 2

    def pair_shapes(blocks):
        return (
            jax.ShapeDtypeStruct((line, blocks * t, r), f32),
            jax.ShapeDtypeStruct((line, blocks * t, r), bf16),
        )

    def pair_sum(keep, give):
        return (keep + give.astype(f32)).astype(bf16)

    back_keep, back_give, token_rows = pl.pallas_call(
        functools.partial(project_cot_kernel, count),
        out_shape=(*pair_shapes(count), jax.ShapeDtypeStruct((peers, t, block), bf16)),
        in_specs=[smem, smem] + [vmem] * (1 + count),
        out_specs=(vmem, vmem, vmem),
        compiler_params=limit(16),
        name="project_cot",
    )(order, spot_ref, rows, *ups)
    back_part = pair_sum(back_keep, pair_swap(back_give))
    far_rows = [chip_shift(token_rows, j) for j in range(1, count // 2)]
    keep, give = pl.pallas_call(
        functools.partial(project_kernel, count),
        out_shape=pair_shapes(2 * count - 1),
        in_specs=[smem, smem] + [vmem] * (1 + 2 * count),
        out_specs=(vmem, vmem),
        compiler_params=limit(16),
        name="project",
    )(order, spot_ref, rows, *downs, *ups)
    got, *far_rows = lax.optimization_barrier((pair_swap(give), *far_rows))
    gram_sum = jnp.sum(packed[:, :gram_rows].astype(f32), axis=0).astype(bf16)
    all_lengths = packed[:, gram_rows, :seqs].astype(jnp.int32)
    own_grams = line_exchange(repeated(gram_sum, line))
    part = jnp.concatenate([pair_sum(keep, got), back_part], axis=1)
    own_grams, part = lax.optimization_barrier((own_grams, part))
    sums = line_exchange(part)
    all_rows = [token_rows, *far_rows]
    all_rows += [core_swap(b) for b in all_rows]
    sums, all_rows = lax.optimization_barrier((sums, all_rows))
    grams = gather_section(own_grams) + gather_section(pair_swap(own_grams))

    own_held, held = pl.pallas_call(
        functools.partial(recur_kernel, count, width),
        out_shape=(
            pltpu.HBM((line, count + 1, t, r), bf16),
            pltpu.HBM((count // 2 - 1, 2, t, r), bf16),
        ),
        in_specs=[smem, smem] + [vmem] * (2 + 2 * count),
        out_specs=(vmem, vmem),
        scratch_shapes=[
            pltpu.VMEM((count, count - 1, peers, r // peers, r), bf16),
            pltpu.VMEM((count, t, r), bf16),
        ],
        compiler_params=limit(16),
        name="recur",
    )(order, spot_ref, sums, kept(square, pltpu.HBM), *[kept(g, pltpu.VMEM) for g in grams])
    gain = lax.dynamic_slice_in_dim(norm_gain, spot * block, block, 1)
    own_held, all_lengths, gain = lax.optimization_barrier((own_held, all_lengths, gain))

    half = count // 2
    own = line_exchange(own_held)
    held = [chip_shift(held[j - 1], j) for j in range(1, half)]
    own, *held = lax.optimization_barrier((own, *held))
    own = [own, pair_swap(own)]
    acts = [x[:, 2:] for x in own]
    states = [[None] * count, [None] * count]
    for j in range(half):
        if j:
            grads = line_exchange(repeated(held[j - 1], line))
            blocks = [[g, chip_shift(a, j)] for g, a in zip([grads, pair_swap(grads)], acts)]
        else:
            blocks = [[x] for x in own]
        for p in range(2):
            states[p][j] = blocks[p]
            states[p][half + j] = [core_swap(x) for x in blocks[p]]
    flat = [x for row in states for parts in row for x in parts]

    chunk = min(r, block)
    fisher = pl.pallas_call(
        functools.partial(fisher_kernel, count, seqs, 1.0 / (row_count * peers)),
        out_shape=jax.ShapeDtypeStruct((block, r), f32),
        in_specs=[smem, smem, smem] + [anywhere] * count + [vmem] * (count + len(flat) + 1),
        out_specs=vmem,
        scratch_shapes=[
            pltpu.VMEM((count, peers, t, block), bf16),
            pltpu.VMEM((r, chunk), f32),
            pltpu.VMEM((peers, row_count, chunk), bf16),
            pltpu.VMEM((peers, seqs * r, row_count), bf16),
            pltpu.SemaphoreType.DMA((count,)),
        ],
        compiler_params=limit(24),
        name="squares",
    )(order, place, all_lengths, *[kept(x, pltpu.HBM) for x in all_rows], *ups, *flat, gain)
    return fisher[None]


def solution(mesh):
    in_specs = (
        P("dp", None),
        P("dp", None),
        P("section", "dp", None),
        P("section", "dp", None),
        P("section", None),
        P("dp", None),
    )
    out_specs = P("section", "dp", None)
    return jax.shard_map(
        per_device, mesh=mesh, in_specs=in_specs, out_specs=out_specs, check_vma=False
    )
```

```python
import functools

import jax
import jax.numpy as jnp
from jax import lax
from jax.experimental import pallas as pl
from jax.experimental.pallas import tpu as pltpu
from jax.sharding import PartitionSpec as P

epsilon = 1e-05
bf16 = jnp.bfloat16
f32 = jnp.float32
MIB = 1024 * 1024


def dot(a, b, ca, cb):
    return lax.dot_general(a, b, (((ca,), (cb,)), ((), ())), preferred_element_type=f32)


def core_swap(x):
    count = lax.axis_size("section")
    return lax.ppermute(x, "section", [(i, i ^ 1) for i in range(count)])


def chip_shift(x, by):
    count = lax.axis_size("section")
    return lax.ppermute(x, "section", [(i, (i - 2 * by) % count) for i in range(count)])


def section_order():
    count = lax.axis_size("section")
    me = lax.axis_index("section")
    same = [(me + 2 * j) % count for j in range(count // 2)]
    other = [((me ^ 1) + 2 * j) % count for j in range(count // 2)]
    return jnp.stack(same + other).astype(jnp.int32)


def gather_section(x):
    count = lax.axis_size("section")
    same = [x] + [chip_shift(x, j) for j in range(1, count // 2)]
    return same + [core_swap(b) for b in same]


def kept(x, space):
    return pltpu.with_memory_space_constraint(x, space)


def pair_swap(x):
    peers = lax.axis_size("dp")
    return lax.ppermute(x, "dp", [(i, i ^ 1) for i in range(peers)])


def line_exchange(x):
    peers = lax.axis_size("dp")
    groups = [list(range(p, peers, 2)) for p in range(2)]
    return lax.all_to_all(x, "dp", 0, 0, axis_index_groups=groups, tiled=True)


def repeated(x, times):
    return jnp.broadcast_to(x[None], (times,) + x.shape)


def gram_pairs(count):
    ups = [(k, count + j) for j in range(count - 1) for k in range(j + 1)]
    listed = []
    for chip in range(count // 2):
        own = [(k, l) for l in (2 * chip, 2 * chip + 1) for k in range(l)]
        spare = 2 * (count - 1) - len(own)
        listed += own + ups[:spare]
        ups = ups[spare:]
    return listed


def prepare_kernel(tokens_ref, cot_ref, rows_ref, held, sems, out_sems):
    peers, rows, block = rows_ref.shape
    t = rows // 2
    start = pl.multiple_of(lax.axis_index("section") * t, t)
    pairs = []
    for n in range(peers):
        for k, ref in enumerate((tokens_ref, cot_ref)):
            source = ref.at[pl.ds(start, t), pl.ds(n * block, block)]
            place = (n, pl.ds(k * t, t))
            pairs.append(
                (
                    pltpu.make_async_copy(source, held.at[place], sems.at[k, n]),
                    pltpu.make_async_copy(held.at[place], rows_ref.at[place], out_sems.at[k, n]),
                )
            )
    for come, _ in pairs:
        come.start()
    for come, leave in pairs:
        come.wait()
        leave.start()
    for _, leave in pairs:
        leave.wait()


def weight_kernel(place, rows_ref, down_ref, gain_ref, square_ref, weight_ref):
    peers, rows, block = rows_ref.shape
    t = rows // 2
    total = jnp.zeros((t, 1), f32)
    for n in range(peers):
        wide = rows_ref[n, :t].astype(f32)
        total = total + jnp.sum(wide * wide, axis=-1, keepdims=True)
    square_ref[...] = total
    gain = gain_ref[...].reshape(block, 1)
    weight_ref[...] = (down_ref[0].astype(f32) * gain).astype(bf16)


def gram_kernel(count, seqs, order, left, right, lengths, *refs):
    ups = refs[:count]
    mine, partner, gram_ref, table = refs[count:]
    peers, rows, r = gram_ref.shape
    core = lax.rem(order[0], 2)
    table[core] = mine[...]
    table[1 - core] = partner[...]
    for i in range(count):
        table[2 + order[i]] = ups[i][...]
    share = r // peers
    for p in range(count - 1):
        out = dot(table[2 + left[p]], table[right[p]], 0, 0).astype(bf16)
        gram_ref[:, p * share : (p + 1) * share] = out.reshape(peers, share, r)
    used = (count - 1) * share
    lane = lax.broadcasted_iota(jnp.int32, (rows - used, r), 1)
    line = jnp.zeros((rows - used, r), f32)
    for q in range(seqs):
        line = jnp.where(lane == q, lengths[0, q].astype(f32), line)
    gram_ref[:, used:] = jnp.broadcast_to(line.astype(bf16)[None], (peers, rows - used, r))


def paired(rows, mine):
    return jnp.concatenate(rows(mine) + rows(1 - mine), axis=0)


def store_pair(keep_ref, send_ref, m, t, out):
    line, _, r = keep_ref.shape
    place = pl.ds(pl.multiple_of(m * t, t), t)
    keep_ref[:, place, :] = out[: line * t].reshape(line, t, r)
    send_ref[:, place, :] = out[line * t :].astype(bf16).reshape(line, t, r)


def project_kernel(count, order, spot, rows_ref, *refs):
    downs = refs[:count]
    ups = refs[count : 2 * count]
    keep_ref, send_ref = refs[2 * count :]
    peers, rows, _ = rows_ref.shape
    t = rows // 2
    x = paired(lambda p: [rows_ref[2 * z + p, :t] for z in range(peers // 2)], lax.rem(spot[0], 2))
    for i in range(count):
        layer = order[i]
        store_pair(keep_ref, send_ref, layer, t, dot(x, downs[i][...], 1, 0))

        @pl.when(layer < count - 1)
        def _():
            store_pair(keep_ref, send_ref, count + layer, t, dot(x, ups[i][...], 1, 0))


def project_cot_kernel(count, order, spot, rows_ref, *refs):
    ups = refs[:count]
    keep_ref, send_ref, tokens_ref = refs[count:]
    peers, rows, _ = rows_ref.shape
    t = rows // 2
    tokens_ref[...] = rows_ref[:, :t]
    c = paired(lambda p: [rows_ref[2 * z + p, t:] for z in range(peers // 2)], lax.rem(spot[0], 2))
    for i in range(count):
        store_pair(keep_ref, send_ref, order[i], t, dot(c, ups[i][...], 1, 0))


def combine_kernel(keep_ref, got_ref, back_keep_ref, back_got_ref, out_ref):
    cut = keep_ref.shape[1]
    out_ref[:, :cut] = (keep_ref[...] + got_ref[...].astype(f32)).astype(bf16)
    out_ref[:, cut:] = (back_keep_ref[...] + back_got_ref[...].astype(f32)).astype(bf16)


def collect_kernel(packed_ref, gram_ref, lengths_ref):
    copies, rows, _ = gram_ref.shape
    total = jnp.sum(packed_ref[:, :rows].astype(f32), axis=0).astype(bf16)
    for z in range(copies):
        gram_ref[z] = total
    for n in range(packed_ref.shape[0]):
        lengths_ref[n : n + 1] = packed_ref[n, rows : rows + 16].astype(f32)[:1]


def recur_kernel(count, width, order, spot, sums_ref, sq_ref, *refs):
    grams = refs[: 2 * count]
    own_ref, out_ref, table, grads = refs[2 * count :]
    copies, _, t, _ = own_ref.shape
    half = count // 2

    def put(m, value):
        for z in range(copies):
            own_ref[z, m] = value

    per = count - 1
    mine = lax.rem(spot[0], 2)
    line = grams[0].shape[0]
    _, _, peers, share, r = table.shape
    for i in range(count):
        for z in range(line):
            for p in range(per):
                rows = slice(p * share, (p + 1) * share)
                table[order[i], p, 2 * z + mine] = grams[i][z, rows]
                table[order[i], p, 2 * z + 1 - mine] = grams[count + i][z, rows]
    place = {pair: n for n, pair in enumerate(gram_pairs(count))}

    def product(pair):
        n = place[pair]
        return table[n // per, n % per].reshape(peers * share, r)

    def mixed(k, l):
        return product((k, l))

    def ups(k, j, a):
        if k <= j:
            return dot(a, product((k, count + j)), 1, 0)
        return dot(a, product((j, count + k)), 1, 1)

    def total(ref, start):
        return jnp.sum(ref[:, start : start + t].astype(f32), axis=0)

    proj = [total(sums_ref, l * t) for l in range(count)]
    hu = [total(sums_ref, (count + k) * t) for k in range(count - 1)]
    back = [total(sums_ref, (2 * count - 1 + l) * t) for l in range(count)]
    norm = sq_ref[...]
    invs, pres, hus = [], [], []
    for l in range(count):
        inv = lax.rsqrt(norm / width + epsilon)
        pre = inv * proj[l]
        invs.append(inv)
        pres.append(pre)
        hus.append(list(hu))
        if l < count - 1:
            act = (pre * jax.nn.sigmoid(pre)).astype(bf16)
            put(2 + l, act)
            wide = act.astype(f32)
            for j in range(l + 1, count):
                proj[j] = proj[j] + dot(act, mixed(l, j), 1, 0)
            step = [ups(l, j, act) for j in range(count - 1)]
            norm = norm + jnp.sum(wide * (2.0 * hu[l] + step[l]), axis=-1, keepdims=True)
            hu = [hu[j] + step[j] for j in range(count - 1)]
    for l in reversed(range(count)):
        s = jax.nn.sigmoid(pres[l])
        grad = (back[l] * s * (1.0 + pres[l] * (1.0 - s))).astype(bf16)
        wide = grad.astype(f32)
        grads[l] = (wide * invs[l]).astype(bf16)
        inner = jnp.sum(wide * proj[l], axis=-1, keepdims=True) / width
        for j in range(l):
            back[j] = back[j] + invs[l] * (
                dot(grad, mixed(j, l), 1, 1) - invs[l] * invs[l] * inner * hus[l][j]
            )
    chip = order[0] // 2
    for m in range(2):
        put(m, grads[2 * chip + m])
        for j in range(1, half):
            out_ref[j - 1, m] = grads[2 * lax.rem(chip + half - j, half) + m]


def fisher_kernel(count, seqs, scale, order, place, *refs):
    half = count // 2
    rows = refs[:count]
    ups = refs[count : 2 * count]
    states = refs[2 * count : 4 * count]
    far_count = 2 * (half - 1)
    apart = refs[4 * count : 4 * count + far_count]
    rest = refs[4 * count + far_count :]
    lengths_ref, gain_ref, out_ref, acc, hidden, masks = rest
    peers, t, width = rows[0].shape
    r = out_ref.shape[1]
    chunk = min(r, width)
    span = count * t
    me = place[0]
    mine = lax.rem(place[1], 2)
    line = peers // 2
    names = [2 * (n % line) + (mine if n < line else 1 - mine) for n in range(peers)]
    spot = lax.broadcasted_iota(jnp.int32, (1, span), 1)
    position = spot
    for i in range(count):
        inside = (spot >= i * t) & (spot < (i + 1) * t)
        position = jnp.where(inside, spot + (order[i] - i) * t, position)
    position = position.astype(f32)

    def grad_rows(n, m):
        found = states[n // line * count :][:count]
        parts = []
        for i in range(count):
            core, j = divmod(i, half)
            parts.append(apart[core * (half - 1) + j - 1][names[n], m] if j else found[i][n % line, m])
        return jnp.concatenate(parts, axis=0)

    def act_rows(n, k):
        found = states[n // line * count :][:count]
        shifts = [0 if i % half else 2 for i in range(count)]
        return jnp.concatenate([found[i][n % line, shifts[i] + k] for i in range(count)], axis=0)

    acts = []
    for i in range(1, count):
        act = jnp.concatenate([act_rows(n, jnp.minimum(order[i], count - 2)) for n in range(peers)], axis=0)
        acts.append(jnp.where(order[i] < me, act, jnp.zeros_like(act)))
    for n in range(peers):
        grad = grad_rows(n, lax.rem(me, 2)).astype(f32).T
        lengths = lengths_ref[pl.ds(names[n], 1)]
        start = jnp.zeros((1, 1), f32)
        for q in range(seqs):
            stop = start + lengths[:, q : q + 1]
            inside = (position >= start) & (position < stop)
            masks[n, q * r : (q + 1) * r] = jnp.where(inside, grad, 0.0).astype(bf16)
            start = stop
    for f in range(width // chunk):
        cols = slice(f * chunk, (f + 1) * chunk)
        update = dot(acts[0], ups[1][cols], 1, 1)
        for i in range(2, count):
            update = update + dot(acts[i - 1], ups[i][cols], 1, 1)
        for n in range(peers):
            h = jnp.concatenate([rows[i][names[n], :, cols] for i in range(count)], axis=0).astype(f32)
            hidden[n] = (h + update[n * span : (n + 1) * span]).astype(bf16)
        for n in range(peers):
            total = None
            for q in range(seqs):
                g = dot(masks[n, q * r : (q + 1) * r], hidden[n], 1, 0)
                total = g * g if total is None else total + g * g
            if n == 0:
                acc[...] = total
            else:
                acc[...] = acc[...] + total
        gain = gain_ref[:, cols]
        out_ref[cols] = (acc[...] * (gain * gain * scale)).T


def per_device(tokens, cotangent, down_weight, up_weight, norm_gain, lengths):
    count = lax.axis_size("section")
    peers = lax.axis_size("dp")
    me = lax.axis_index("section")
    spot = lax.axis_index("dp")
    row_count, width = tokens.shape
    block = width // peers
    t = row_count // count
    r = down_weight.shape[2]
    order = section_order()
    smem = pl.BlockSpec(memory_space=pltpu.SMEM)
    vmem = pl.BlockSpec(memory_space=pltpu.VMEM)
    anywhere = pl.BlockSpec(memory_space=pl.ANY)

    def limit(mib):
        return pltpu.CompilerParams(vmem_limit_bytes=mib * MIB)

    place = jnp.stack([me, spot]).astype(jnp.int32)
    spot_ref = place[1:]
    ups = gather_section(up_weight[0])
    send = pl.pallas_call(
        prepare_kernel,
        out_shape=pltpu.HBM((peers, 2 * t, block), bf16),
        in_specs=[anywhere, anywhere],
        out_specs=anywhere,
        scratch_shapes=[
            pltpu.VMEM((peers, 2 * t, block), bf16),
            pltpu.SemaphoreType.DMA((2, peers)),
            pltpu.SemaphoreType.DMA((2, peers)),
        ],
        name="prepare",
    )(tokens, cotangent)
    square, weight = pl.pallas_call(
        weight_kernel,
        grid_spec=pltpu.PrefetchScalarGridSpec(
            num_scalar_prefetch=1,
            grid=(1,),
            in_specs=[
                pl.BlockSpec((peers, 2 * t, block), lambda n, place: (0, 0, 0)),
                pl.BlockSpec((1, block, r), lambda n, place: (0, 0, 0)),
                pl.BlockSpec((1, block), lambda n, place: (0, place[1])),
            ],
            out_specs=[
                pl.BlockSpec((t, 1), lambda n, place: (0, 0)),
                pl.BlockSpec((block, r), lambda n, place: (0, 0)),
            ],
        ),
        out_shape=(
            jax.ShapeDtypeStruct((t, 1), f32),
            jax.ShapeDtypeStruct((block, r), bf16),
        ),
        compiler_params=limit(12),
        name="weight",
    )(place, send, down_weight, norm_gain)
    partner = core_swap(weight)
    rows = lax.all_to_all(send, "dp", 0, 0, tiled=True)

    pairs = gram_pairs(count)
    left = lax.dynamic_slice_in_dim(jnp.array([a for a, _ in pairs], jnp.int32), me * (count - 1), count - 1)
    codes = jnp.array([b % 2 if b < count else 2 + b - count for _, b in pairs], jnp.int32)
    right = lax.dynamic_slice_in_dim(codes, me * (count - 1), count - 1)
    seqs = lengths.shape[1]
    gram_rows = (count - 1) * (r // peers)
    packed = pl.pallas_call(
        functools.partial(gram_kernel, count, seqs),
        out_shape=jax.ShapeDtypeStruct((peers, gram_rows + 16, r), bf16),
        in_specs=[smem] * 4 + [vmem] * (count + 2),
        out_specs=vmem,
        scratch_shapes=[pltpu.VMEM((2 + count, block, r), bf16)],
        compiler_params=limit(16),
        name="gram",
    )(order, left, right, lengths, *ups, weight, partner)
    packed, weight = lax.optimization_barrier((packed, weight))
    far = [chip_shift(weight, j) for j in range(1, count // 2)]

    packed = lax.all_to_all(packed, "dp", 0, 0, tiled=True)

    line = peers // 2

    def pair_shapes(blocks):
        return (
            pltpu.HBM((line, blocks * t, r), f32),
            pltpu.HBM((line, blocks * t, r), bf16),
        )

    back_keep, back_give, token_rows = pl.pallas_call(
        functools.partial(project_cot_kernel, count),
        out_shape=(*pair_shapes(count), jax.ShapeDtypeStruct((peers, t, block), bf16)),
        in_specs=[smem, smem] + [vmem] * (1 + count),
        out_specs=(vmem, vmem, vmem),
        compiler_params=limit(16),
        name="project_cot",
    )(order, spot_ref, rows, *ups)
    back_got = pair_swap(back_give)
    back_keep, *far = lax.optimization_barrier((back_keep, *far))
    downs = [weight, *far, partner, *[core_swap(b) for b in far]]
    far_rows = [chip_shift(token_rows, j) for j in range(1, count // 2)]
    keep, give = pl.pallas_call(
        functools.partial(project_kernel, count),
        out_shape=pair_shapes(2 * count - 1),
        in_specs=[smem, smem] + [vmem] * (1 + 2 * count),
        out_specs=(vmem, vmem),
        compiler_params=limit(16),
        name="project",
    )(order, spot_ref, rows, *downs, *ups)
    got, *far_rows = lax.optimization_barrier((pair_swap(give), *far_rows))
    gram_sums, all_lengths = pl.pallas_call(
        collect_kernel,
        out_shape=(pltpu.HBM((line, gram_rows, r), bf16), jax.ShapeDtypeStruct((peers, r), f32)),
        in_specs=[vmem],
        out_specs=(vmem, vmem),
        compiler_params=limit(8),
        name="collect",
    )(packed)
    gram_sums, back_got = lax.optimization_barrier((gram_sums, back_got))
    own_grams = line_exchange(gram_sums)
    part = pl.pallas_call(
        combine_kernel,
        out_shape=pltpu.HBM((line, (3 * count - 1) * t, r), bf16),
        in_specs=[vmem] * 4,
        out_specs=vmem,
        compiler_params=limit(12),
        name="combine",
    )(kept(keep, pltpu.HBM), got, kept(back_keep, pltpu.HBM), back_got)
    own_grams, part = lax.optimization_barrier((own_grams, part))
    sums = line_exchange(part)
    all_rows = [token_rows, *far_rows]
    all_rows += [core_swap(b) for b in all_rows]
    sums, all_rows = lax.optimization_barrier((sums, all_rows))
    grams = gather_section(own_grams) + gather_section(pair_swap(own_grams))

    own_held, held = pl.pallas_call(
        functools.partial(recur_kernel, count, width),
        out_shape=(
            pltpu.HBM((line, count + 1, t, r), bf16),
            pltpu.HBM((count // 2 - 1, 2, t, r), bf16),
        ),
        in_specs=[smem, smem] + [vmem] * (2 + 2 * count),
        out_specs=(vmem, vmem),
        scratch_shapes=[
            pltpu.VMEM((count, count - 1, peers, r // peers, r), bf16),
            pltpu.VMEM((count, t, r), bf16),
        ],
        compiler_params=limit(16),
        name="recur",
    )(order, spot_ref, sums, kept(square, pltpu.HBM), *[kept(g, pltpu.VMEM) for g in grams])
    gain = lax.dynamic_slice_in_dim(norm_gain, spot * block, block, 1)
    own_held, all_lengths, gain = lax.optimization_barrier((own_held, all_lengths, gain))

    half = count // 2
    own = line_exchange(own_held)
    far = [repeated(chip_shift(held[j - 1], j), peers) for j in range(1, half)]
    acts = own[:, 2:]
    own, acts, *far = lax.optimization_barrier((own, acts, *far))
    own = [own, pair_swap(own)]
    acts = [acts, own[1][:, 2:]]
    mine = [lax.all_to_all(x, "dp", 0, 0, tiled=True) for x in far]
    grads = [*mine, *[core_swap(x) for x in mine]]
    states = []
    for p in range(2):
        blocks = [own[p], *[chip_shift(acts[p], j) for j in range(1, half)]]
        states += [*blocks, *[core_swap(x) for x in blocks]]
    flat = [*states, *grads]

    chunk = min(r, block)
    fisher = pl.pallas_call(
        functools.partial(fisher_kernel, count, seqs, 1.0 / (row_count * peers)),
        out_shape=jax.ShapeDtypeStruct((block, r), f32),
        in_specs=[smem, smem] + [vmem] * (2 * count + len(flat) + 2),
        out_specs=vmem,
        scratch_shapes=[
            pltpu.VMEM((r, chunk), f32),
            pltpu.VMEM((peers, row_count, chunk), bf16),
            pltpu.VMEM((peers, seqs * r, row_count), bf16),
        ],
        compiler_params=limit(24),
        name="squares",
    )(order, place, *all_rows, *ups, *flat, all_lengths, gain)
    return fisher[None]


def solution(mesh):
    in_specs = (
        P("dp", None),
        P("dp", None),
        P("section", "dp", None),
        P("section", "dp", None),
        P("section", None),
        P("dp", None),
    )
    out_specs = P("section", "dp", None)
    return jax.shard_map(
        per_device, mesh=mesh, in_specs=in_specs, out_specs=out_specs, check_vma=False
    )
```

```python
import functools

import jax
import jax.numpy as jnp
from jax import lax
from jax.experimental import pallas as pl
from jax.experimental.pallas import tpu as pltpu
from jax.sharding import PartitionSpec as P

epsilon = 1e-05
bf16 = jnp.bfloat16
f32 = jnp.float32
MIB = 1024 * 1024


def dot(a, b, ca, cb):
    return lax.dot_general(a, b, (((ca,), (cb,)), ((), ())), preferred_element_type=f32)


def core_swap(x):
    count = lax.axis_size("section")
    return lax.ppermute(x, "section", [(i, i ^ 1) for i in range(count)])


def chip_shift(x, by):
    count = lax.axis_size("section")
    return lax.ppermute(x, "section", [(i, (i - 2 * by) % count) for i in range(count)])


def section_order():
    count = lax.axis_size("section")
    me = lax.axis_index("section")
    same = [(me + 2 * j) % count for j in range(count // 2)]
    other = [((me ^ 1) + 2 * j) % count for j in range(count // 2)]
    return jnp.stack(same + other).astype(jnp.int32)


def gather_section(x):
    count = lax.axis_size("section")
    same = [x] + [chip_shift(x, j) for j in range(1, count // 2)]
    return same + [core_swap(b) for b in same]


def kept(x, space):
    return pltpu.with_memory_space_constraint(x, space)


def pair_swap(x):
    peers = lax.axis_size("dp")
    return lax.ppermute(x, "dp", [(i, i ^ 1) for i in range(peers)])


def line_exchange(x):
    peers = lax.axis_size("dp")
    groups = [list(range(p, peers, 2)) for p in range(2)]
    return lax.all_to_all(x, "dp", 0, 0, axis_index_groups=groups, tiled=True)


def repeated(x, times):
    return jnp.broadcast_to(x[None], (times,) + x.shape)


def gram_pairs(count):
    ups = [(k, count + j) for j in range(count - 1) for k in range(j + 1)]
    listed = []
    for chip in range(count // 2):
        own = [(k, l) for l in (2 * chip, 2 * chip + 1) for k in range(l)]
        spare = 2 * (count - 1) - len(own)
        listed += own + ups[:spare]
        ups = ups[spare:]
    return listed


def prepare_kernel(tokens_ref, cot_ref, rows_ref, held, sems, out_sems):
    peers, rows, block = rows_ref.shape
    t = rows // 2
    start = pl.multiple_of(lax.axis_index("section") * t, t)
    pairs = []
    for n in range(peers):
        for k, ref in enumerate((tokens_ref, cot_ref)):
            source = ref.at[pl.ds(start, t), pl.ds(n * block, block)]
            place = (n, pl.ds(k * t, t))
            pairs.append(
                (
                    pltpu.make_async_copy(source, held.at[place], sems.at[k, n]),
                    pltpu.make_async_copy(held.at[place], rows_ref.at[place], out_sems.at[k, n]),
                )
            )
    for come, _ in pairs:
        come.start()
    for come, leave in pairs:
        come.wait()
        leave.start()
    for _, leave in pairs:
        leave.wait()


def weight_kernel(place, rows_ref, down_ref, gain_ref, square_ref, weight_ref):
    peers, rows, block = rows_ref.shape
    t = rows // 2
    total = jnp.zeros((t, 1), f32)
    for n in range(peers):
        wide = rows_ref[n, :t].astype(f32)
        total = total + jnp.sum(wide * wide, axis=-1, keepdims=True)
    square_ref[...] = total
    gain = gain_ref[...].reshape(block, 1)
    weight_ref[...] = (down_ref[0].astype(f32) * gain).astype(bf16)


def gram_kernel(count, seqs, order, left, right, lengths, *refs):
    ups = refs[:count]
    mine, partner, gram_ref, table = refs[count:]
    peers, rows, r = gram_ref.shape
    core = lax.rem(order[0], 2)
    table[core] = mine[...]
    table[1 - core] = partner[...]
    for i in range(count):
        table[2 + order[i]] = ups[i][...]
    share = r // peers
    for p in range(count - 1):
        out = dot(table[2 + left[p]], table[right[p]], 0, 0).astype(bf16)
        gram_ref[:, p * share : (p + 1) * share] = out.reshape(peers, share, r)
    used = (count - 1) * share
    lane = lax.broadcasted_iota(jnp.int32, (rows - used, r), 1)
    line = jnp.zeros((rows - used, r), f32)
    for q in range(seqs):
        line = jnp.where(lane == q, lengths[0, q].astype(f32), line)
    gram_ref[:, used:] = jnp.broadcast_to(line.astype(bf16)[None], (peers, rows - used, r))


def paired(rows, mine):
    return jnp.concatenate(rows(mine) + rows(1 - mine), axis=0)


def store_pair(keep_ref, send_ref, m, t, out):
    line, _, r = keep_ref.shape
    place = pl.ds(pl.multiple_of(m * t, t), t)
    keep_ref[:, place, :] = out[: line * t].reshape(line, t, r)
    send_ref[:, place, :] = out[line * t :].astype(bf16).reshape(line, t, r)


def project_kernel(count, order, spot, rows_ref, *refs):
    downs = refs[:count]
    ups = refs[count : 2 * count]
    keep_ref, send_ref = refs[2 * count :]
    peers, rows, _ = rows_ref.shape
    t = rows // 2
    x = paired(lambda p: [rows_ref[2 * z + p, :t] for z in range(peers // 2)], lax.rem(spot[0], 2))
    for i in range(count):
        layer = order[i]
        store_pair(keep_ref, send_ref, layer, t, dot(x, downs[i][...], 1, 0))

        @pl.when(layer < count - 1)
        def _():
            store_pair(keep_ref, send_ref, count + layer, t, dot(x, ups[i][...], 1, 0))


def project_cot_kernel(count, order, spot, rows_ref, *refs):
    ups = refs[:count]
    keep_ref, send_ref, tokens_ref = refs[count:]
    peers, rows, _ = rows_ref.shape
    t = rows // 2
    tokens_ref[...] = rows_ref[:, :t]
    c = paired(lambda p: [rows_ref[2 * z + p, t:] for z in range(peers // 2)], lax.rem(spot[0], 2))
    for i in range(count):
        store_pair(keep_ref, send_ref, order[i], t, dot(c, ups[i][...], 1, 0))


def combine_kernel(keep_ref, got_ref, back_keep_ref, back_got_ref, out_ref):
    cut = keep_ref.shape[1]
    out_ref[:, :cut] = (keep_ref[...] + got_ref[...].astype(f32)).astype(bf16)
    out_ref[:, cut:] = (back_keep_ref[...] + back_got_ref[...].astype(f32)).astype(bf16)


def collect_kernel(packed_ref, gram_ref, lengths_ref):
    copies, rows, _ = gram_ref.shape
    total = jnp.sum(packed_ref[:, :rows].astype(f32), axis=0).astype(bf16)
    for z in range(copies):
        gram_ref[z] = total
    for n in range(packed_ref.shape[0]):
        lengths_ref[n : n + 1] = packed_ref[n, rows : rows + 16].astype(f32)[:1]


def recur_kernel(count, width, order, spot, sums_ref, sq_ref, *refs):
    grams = refs[: 2 * count]
    own_ref, out_ref, table, grads = refs[2 * count :]
    copies, _, t, _ = own_ref.shape
    half = count // 2

    def put(m, value):
        for z in range(copies):
            own_ref[z, m] = value

    per = count - 1
    mine = lax.rem(spot[0], 2)
    line = grams[0].shape[0]
    _, _, peers, share, r = table.shape
    for i in range(count):
        for z in range(line):
            for p in range(per):
                rows = slice(p * share, (p + 1) * share)
                table[order[i], p, 2 * z + mine] = grams[i][z, rows]
                table[order[i], p, 2 * z + 1 - mine] = grams[count + i][z, rows]
    place = {pair: n for n, pair in enumerate(gram_pairs(count))}

    def product(pair):
        n = place[pair]
        return table[n // per, n % per].reshape(peers * share, r)

    def mixed(k, l):
        return product((k, l))

    def ups(k, j, a):
        if k <= j:
            return dot(a, product((k, count + j)), 1, 0)
        return dot(a, product((j, count + k)), 1, 1)

    def total(ref, start):
        return jnp.sum(ref[:, start : start + t].astype(f32), axis=0)

    proj = [total(sums_ref, l * t) for l in range(count)]
    hu = [total(sums_ref, (count + k) * t) for k in range(count - 1)]
    back = [total(sums_ref, (2 * count - 1 + l) * t) for l in range(count)]
    norm = sq_ref[...]
    invs, pres, hus = [], [], []
    for l in range(count):
        inv = lax.rsqrt(norm / width + epsilon)
        pre = inv * proj[l]
        invs.append(inv)
        pres.append(pre)
        hus.append(list(hu))
        if l < count - 1:
            act = (pre * jax.nn.sigmoid(pre)).astype(bf16)
            put(2 + l, act)
            wide = act.astype(f32)
            for j in range(l + 1, count):
                proj[j] = proj[j] + dot(act, mixed(l, j), 1, 0)
            step = [ups(l, j, act) for j in range(count - 1)]
            norm = norm + jnp.sum(wide * (2.0 * hu[l] + step[l]), axis=-1, keepdims=True)
            hu = [hu[j] + step[j] for j in range(count - 1)]
    for l in reversed(range(count)):
        s = jax.nn.sigmoid(pres[l])
        grad = (back[l] * s * (1.0 + pres[l] * (1.0 - s))).astype(bf16)
        wide = grad.astype(f32)
        grads[l] = (wide * invs[l]).astype(bf16)
        inner = jnp.sum(wide * proj[l], axis=-1, keepdims=True) / width
        for j in range(l):
            back[j] = back[j] + invs[l] * (
                dot(grad, mixed(j, l), 1, 1) - invs[l] * invs[l] * inner * hus[l][j]
            )
    chip = order[0] // 2
    for m in range(2):
        put(m, grads[2 * chip + m])
        for j in range(1, half):
            out_ref[j - 1, m] = grads[2 * lax.rem(chip + half - j, half) + m]


def fisher_kernel(count, seqs, scale, order, place, *refs):
    half = count // 2
    rows = refs[:count]
    ups = refs[count : 2 * count]
    states = refs[2 * count : 4 * count]
    far_count = 2 * (half - 1)
    apart = refs[4 * count : 4 * count + far_count]
    rest = refs[4 * count + far_count :]
    lengths_ref, gain_ref, out_ref, acc, hidden, masks = rest
    peers, t, width = rows[0].shape
    r = out_ref.shape[1]
    chunk = min(r, width)
    span = count * t
    me = place[0]
    mine = lax.rem(place[1], 2)
    line = peers // 2
    names = [2 * (n % line) + (mine if n < line else 1 - mine) for n in range(peers)]
    spot = lax.broadcasted_iota(jnp.int32, (1, span), 1)
    position = spot
    for i in range(count):
        inside = (spot >= i * t) & (spot < (i + 1) * t)
        position = jnp.where(inside, spot + (order[i] - i) * t, position)
    position = position.astype(f32)

    def grad_rows(n, m):
        found = states[n // line * count :][:count]
        parts = []
        for i in range(count):
            core, j = divmod(i, half)
            parts.append(apart[core * (half - 1) + j - 1][names[n], m] if j else found[i][n % line, m])
        return jnp.concatenate(parts, axis=0)

    def act_rows(n, k):
        found = states[n // line * count :][:count]
        shifts = [0 if i % half else 2 for i in range(count)]
        return jnp.concatenate([found[i][n % line, shifts[i] + k] for i in range(count)], axis=0)

    acts = []
    for i in range(1, count):
        act = jnp.concatenate([act_rows(n, jnp.minimum(order[i], count - 2)) for n in range(peers)], axis=0)
        acts.append(jnp.where(order[i] < me, act, jnp.zeros_like(act)))
    for n in range(peers):
        grad = grad_rows(n, lax.rem(me, 2)).astype(f32).T
        lengths = lengths_ref[pl.ds(names[n], 1)]
        start = jnp.zeros((1, 1), f32)
        for q in range(seqs):
            stop = start + lengths[:, q : q + 1]
            inside = (position >= start) & (position < stop)
            masks[n, q * r : (q + 1) * r] = jnp.where(inside, grad, 0.0).astype(bf16)
            start = stop
    for f in range(width // chunk):
        cols = slice(f * chunk, (f + 1) * chunk)
        update = dot(acts[0], ups[1][cols], 1, 1)
        for i in range(2, count):
            update = update + dot(acts[i - 1], ups[i][cols], 1, 1)
        for n in range(peers):
            h = jnp.concatenate([rows[i][names[n], :, cols] for i in range(count)], axis=0).astype(f32)
            hidden[n] = (h + update[n * span : (n + 1) * span]).astype(bf16)
        for n in range(peers):
            total = None
            for q in range(seqs):
                g = dot(masks[n, q * r : (q + 1) * r], hidden[n], 1, 0)
                total = g * g if total is None else total + g * g
            if n == 0:
                acc[...] = total
            else:
                acc[...] = acc[...] + total
        gain = gain_ref[:, cols]
        out_ref[cols] = (acc[...] * (gain * gain * scale)).T


def per_device(tokens, cotangent, down_weight, up_weight, norm_gain, lengths):
    count = lax.axis_size("section")
    peers = lax.axis_size("dp")
    me = lax.axis_index("section")
    spot = lax.axis_index("dp")
    row_count, width = tokens.shape
    block = width // peers
    t = row_count // count
    r = down_weight.shape[2]
    order = section_order()
    smem = pl.BlockSpec(memory_space=pltpu.SMEM)
    vmem = pl.BlockSpec(memory_space=pltpu.VMEM)
    anywhere = pl.BlockSpec(memory_space=pl.ANY)

    def limit(mib):
        return pltpu.CompilerParams(vmem_limit_bytes=mib * MIB)

    place = jnp.stack([me, spot]).astype(jnp.int32)
    spot_ref = place[1:]
    ups = gather_section(up_weight[0])
    send = pl.pallas_call(
        prepare_kernel,
        out_shape=pltpu.HBM((peers, 2 * t, block), bf16),
        in_specs=[anywhere, anywhere],
        out_specs=anywhere,
        scratch_shapes=[
            pltpu.VMEM((peers, 2 * t, block), bf16),
            pltpu.SemaphoreType.DMA((2, peers)),
            pltpu.SemaphoreType.DMA((2, peers)),
        ],
        name="prepare",
    )(tokens, cotangent)
    square, weight = pl.pallas_call(
        weight_kernel,
        grid_spec=pltpu.PrefetchScalarGridSpec(
            num_scalar_prefetch=1,
            grid=(1,),
            in_specs=[
                pl.BlockSpec((peers, 2 * t, block), lambda n, place: (0, 0, 0)),
                pl.BlockSpec((1, block, r), lambda n, place: (0, 0, 0)),
                pl.BlockSpec((1, block), lambda n, place: (0, place[1])),
            ],
            out_specs=[
                pl.BlockSpec((t, 1), lambda n, place: (0, 0)),
                pl.BlockSpec((block, r), lambda n, place: (0, 0)),
            ],
        ),
        out_shape=(
            jax.ShapeDtypeStruct((t, 1), f32),
            jax.ShapeDtypeStruct((block, r), bf16),
        ),
        compiler_params=limit(12),
        name="weight",
    )(place, send, down_weight, norm_gain)
    partner = core_swap(weight)
    rows = lax.all_to_all(send, "dp", 0, 0, tiled=True)

    pairs = gram_pairs(count)
    left = lax.dynamic_slice_in_dim(jnp.array([a for a, _ in pairs], jnp.int32), me * (count - 1), count - 1)
    codes = jnp.array([b % 2 if b < count else 2 + b - count for _, b in pairs], jnp.int32)
    right = lax.dynamic_slice_in_dim(codes, me * (count - 1), count - 1)
    seqs = lengths.shape[1]
    gram_rows = (count - 1) * (r // peers)
    packed = pl.pallas_call(
        functools.partial(gram_kernel, count, seqs),
        out_shape=jax.ShapeDtypeStruct((peers, gram_rows + 16, r), bf16),
        in_specs=[smem] * 4 + [vmem] * (count + 2),
        out_specs=vmem,
        scratch_shapes=[pltpu.VMEM((2 + count, block, r), bf16)],
        compiler_params=limit(16),
        name="gram",
    )(order, left, right, lengths, *ups, weight, partner)
    packed, weight = lax.optimization_barrier((packed, weight))
    far = [chip_shift(weight, j) for j in range(1, count // 2)]

    packed = lax.all_to_all(packed, "dp", 0, 0, tiled=True)

    line = peers // 2

    def pair_shapes(blocks):
        return (
            pltpu.HBM((line, blocks * t, r), f32),
            pltpu.HBM((line, blocks * t, r), bf16),
        )

    back_keep, back_give, token_rows = pl.pallas_call(
        functools.partial(project_cot_kernel, count),
        out_shape=(*pair_shapes(count), jax.ShapeDtypeStruct((peers, t, block), bf16)),
        in_specs=[smem, smem] + [vmem] * (1 + count),
        out_specs=(vmem, vmem, vmem),
        compiler_params=limit(16),
        name="project_cot",
    )(order, spot_ref, rows, *ups)
    back_got = pair_swap(back_give)
    back_keep, *far = lax.optimization_barrier((back_keep, *far))
    downs = [weight, *far, partner, *[core_swap(b) for b in far]]
    far_rows = [chip_shift(token_rows, j) for j in range(1, count // 2)]
    keep, give = pl.pallas_call(
        functools.partial(project_kernel, count),
        out_shape=pair_shapes(2 * count - 1),
        in_specs=[smem, smem] + [vmem] * (1 + 2 * count),
        out_specs=(vmem, vmem),
        compiler_params=limit(16),
        name="project",
    )(order, spot_ref, rows, *downs, *ups)
    got, *far_rows = lax.optimization_barrier((pair_swap(give), *far_rows))
    gram_sums, all_lengths = pl.pallas_call(
        collect_kernel,
        out_shape=(pltpu.HBM((line, gram_rows, r), bf16), jax.ShapeDtypeStruct((peers, r), f32)),
        in_specs=[vmem],
        out_specs=(vmem, vmem),
        compiler_params=limit(8),
        name="collect",
    )(packed)
    gram_sums, back_got = lax.optimization_barrier((gram_sums, back_got))
    own_grams = line_exchange(gram_sums)
    part = pl.pallas_call(
        combine_kernel,
        out_shape=pltpu.HBM((line, (3 * count - 1) * t, r), bf16),
        in_specs=[vmem] * 4,
        out_specs=vmem,
        compiler_params=limit(12),
        name="combine",
    )(kept(keep, pltpu.HBM), got, kept(back_keep, pltpu.HBM), back_got)
    own_grams, part = lax.optimization_barrier((own_grams, part))
    sums = line_exchange(part)
    all_rows = [token_rows, *far_rows]
    all_rows += [core_swap(b) for b in all_rows]
    sums, all_rows = lax.optimization_barrier((sums, all_rows))
    grams = gather_section(own_grams) + gather_section(pair_swap(own_grams))

    own_held, held = pl.pallas_call(
        functools.partial(recur_kernel, count, width),
        out_shape=(
            pltpu.HBM((line, count + 1, t, r), bf16),
            pltpu.HBM((count // 2 - 1, 2, t, r), bf16),
        ),
        in_specs=[smem, smem] + [vmem] * (2 + 2 * count),
        out_specs=(vmem, vmem),
        scratch_shapes=[
            pltpu.VMEM((count, count - 1, peers, r // peers, r), bf16),
            pltpu.VMEM((count, t, r), bf16),
        ],
        compiler_params=limit(16),
        name="recur",
    )(order, spot_ref, sums, kept(square, pltpu.HBM), *[kept(g, pltpu.VMEM) for g in grams])
    gain = lax.dynamic_slice_in_dim(norm_gain, spot * block, block, 1)
    own_held, all_lengths, gain = lax.optimization_barrier((own_held, all_lengths, gain))

    half = count // 2
    own = line_exchange(own_held)
    far = [repeated(chip_shift(held[j - 1], j), peers) for j in range(1, half)]
    own, *far = lax.optimization_barrier((own, *far))
    own = [own, pair_swap(own)]
    acts = [x[:, 2:] for x in own]
    mine = [lax.all_to_all(x, "dp", 0, 0, tiled=True) for x in far]
    grads = [*mine, *[core_swap(x) for x in mine]]
    states = []
    for p in range(2):
        blocks = [own[p], *[chip_shift(acts[p], j) for j in range(1, half)]]
        states += [*blocks, *[core_swap(x) for x in blocks]]
    flat = [*states, *grads]

    chunk = min(r, block)
    fisher = pl.pallas_call(
        functools.partial(fisher_kernel, count, seqs, 1.0 / (row_count * peers)),
        out_shape=jax.ShapeDtypeStruct((block, r), f32),
        in_specs=[smem, smem] + [vmem] * (2 * count + len(flat) + 2),
        out_specs=vmem,
        scratch_shapes=[
            pltpu.VMEM((r, chunk), f32),
            pltpu.VMEM((peers, row_count, chunk), bf16),
            pltpu.VMEM((peers, seqs * r, row_count), bf16),
        ],
        compiler_params=limit(24),
        name="squares",
    )(order, place, *all_rows, *ups, *flat, all_lengths, gain)
    return fisher[None]


def solution(mesh):
    in_specs = (
        P("dp", None),
        P("dp", None),
        P("section", "dp", None),
        P("section", "dp", None),
        P("section", None),
        P("dp", None),
    )
    out_specs = P("section", "dp", None)
    return jax.shard_map(
        per_device, mesh=mesh, in_specs=in_specs, out_specs=out_specs, check_vma=False
    )
```

```python
import functools

import jax
import jax.numpy as jnp
from jax import lax
from jax.experimental import pallas as pl
from jax.experimental.pallas import tpu as pltpu
from jax.sharding import PartitionSpec as P

epsilon = 1e-05
bf16 = jnp.bfloat16
f32 = jnp.float32
MIB = 1024 * 1024


def dot(a, b, ca, cb):
    return lax.dot_general(a, b, (((ca,), (cb,)), ((), ())), preferred_element_type=f32)


def core_swap(x):
    count = lax.axis_size("section")
    return lax.ppermute(x, "section", [(i, i ^ 1) for i in range(count)])


def chip_shift(x, by):
    count = lax.axis_size("section")
    return lax.ppermute(x, "section", [(i, (i - 2 * by) % count) for i in range(count)])


def section_order():
    count = lax.axis_size("section")
    me = lax.axis_index("section")
    same = [(me + 2 * j) % count for j in range(count // 2)]
    other = [((me ^ 1) + 2 * j) % count for j in range(count // 2)]
    return jnp.stack(same + other).astype(jnp.int32)


def gather_section(x):
    count = lax.axis_size("section")
    same = [x] + [chip_shift(x, j) for j in range(1, count // 2)]
    return same + [core_swap(b) for b in same]


def kept(x, space):
    return pltpu.with_memory_space_constraint(x, space)


def pair_swap(x):
    peers = lax.axis_size("dp")
    return lax.ppermute(x, "dp", [(i, i ^ 1) for i in range(peers)])


def line_exchange(x):
    peers = lax.axis_size("dp")
    groups = [list(range(p, peers, 2)) for p in range(2)]
    return lax.all_to_all(x, "dp", 0, 0, axis_index_groups=groups, tiled=True)


def repeated(x, times):
    return jnp.broadcast_to(x[None], (times,) + x.shape)


def gram_pairs(count):
    ups = [(k, count + j) for j in range(count - 1) for k in range(j + 1)]
    listed = []
    for chip in range(count // 2):
        own = [(k, l) for l in (2 * chip, 2 * chip + 1) for k in range(l)]
        spare = 2 * (count - 1) - len(own)
        listed += own + ups[:spare]
        ups = ups[spare:]
    return listed


def prepare_kernel(tokens_ref, cot_ref, rows_ref, held, sems, out_sems):
    peers, rows, block = rows_ref.shape
    t = rows // 2
    start = pl.multiple_of(lax.axis_index("section") * t, t)
    pairs = []
    for n in range(peers):
        for k, ref in enumerate((tokens_ref, cot_ref)):
            source = ref.at[pl.ds(start, t), pl.ds(n * block, block)]
            place = (n, pl.ds(k * t, t))
            pairs.append(
                (
                    pltpu.make_async_copy(source, held.at[place], sems.at[k, n]),
                    pltpu.make_async_copy(held.at[place], rows_ref.at[place], out_sems.at[k, n]),
                )
            )
    for come, _ in pairs:
        come.start()
    for come, leave in pairs:
        come.wait()
        leave.start()
    for _, leave in pairs:
        leave.wait()


def weight_kernel(place, rows_ref, down_ref, gain_ref, square_ref, weight_ref):
    peers, rows, block = rows_ref.shape
    t = rows // 2
    total = jnp.zeros((t, 1), f32)
    for n in range(peers):
        wide = rows_ref[n, :t].astype(f32)
        total = total + jnp.sum(wide * wide, axis=-1, keepdims=True)
    square_ref[...] = total
    gain = gain_ref[...].reshape(block, 1)
    weight_ref[...] = (down_ref[0].astype(f32) * gain).astype(bf16)


def gram_kernel(count, seqs, order, left, right, lengths, *refs):
    ups = refs[:count]
    mine, partner, gram_ref, table = refs[count:]
    peers, rows, r = gram_ref.shape
    core = lax.rem(order[0], 2)
    table[core] = mine[...]
    table[1 - core] = partner[...]
    for i in range(count):
        table[2 + order[i]] = ups[i][...]
    share = r // peers
    for p in range(count - 1):
        out = dot(table[2 + left[p]], table[right[p]], 0, 0).astype(bf16)
        gram_ref[:, p * share : (p + 1) * share] = out.reshape(peers, share, r)
    used = (count - 1) * share
    lane = lax.broadcasted_iota(jnp.int32, (rows - used, r), 1)
    line = jnp.zeros((rows - used, r), f32)
    for q in range(seqs):
        line = jnp.where(lane == q, lengths[0, q].astype(f32), line)
    gram_ref[:, used:] = jnp.broadcast_to(line.astype(bf16)[None], (peers, rows - used, r))


def paired(rows, mine):
    return jnp.concatenate(rows(mine) + rows(1 - mine), axis=0)


def store_pair(keep_ref, send_ref, m, t, out):
    line, _, r = keep_ref.shape
    place = pl.ds(pl.multiple_of(m * t, t), t)
    keep_ref[:, place, :] = out[: line * t].reshape(line, t, r)
    send_ref[:, place, :] = out[line * t :].astype(bf16).reshape(line, t, r)


def project_kernel(count, order, spot, rows_ref, *refs):
    downs = refs[:count]
    ups = refs[count : 2 * count]
    keep_ref, send_ref = refs[2 * count :]
    peers, rows, _ = rows_ref.shape
    t = rows // 2
    x = paired(lambda p: [rows_ref[2 * z + p, :t] for z in range(peers // 2)], lax.rem(spot[0], 2))
    for i in range(count):
        layer = order[i]
        store_pair(keep_ref, send_ref, layer, t, dot(x, downs[i][...], 1, 0))

        @pl.when(layer < count - 1)
        def _():
            store_pair(keep_ref, send_ref, count + layer, t, dot(x, ups[i][...], 1, 0))


def project_cot_kernel(count, order, spot, rows_ref, *refs):
    ups = refs[:count]
    keep_ref, send_ref, tokens_ref = refs[count:]
    peers, rows, _ = rows_ref.shape
    t = rows // 2
    tokens_ref[...] = rows_ref[:, :t]
    c = paired(lambda p: [rows_ref[2 * z + p, t:] for z in range(peers // 2)], lax.rem(spot[0], 2))
    for i in range(count):
        store_pair(keep_ref, send_ref, order[i], t, dot(c, ups[i][...], 1, 0))


def combine_kernel(keep_ref, got_ref, back_keep_ref, back_got_ref, out_ref):
    cut = keep_ref.shape[1]
    out_ref[:, :cut] = (keep_ref[...] + got_ref[...].astype(f32)).astype(bf16)
    out_ref[:, cut:] = (back_keep_ref[...] + back_got_ref[...].astype(f32)).astype(bf16)


def collect_kernel(packed_ref, gram_ref, lengths_ref):
    copies, rows, _ = gram_ref.shape
    total = jnp.sum(packed_ref[:, :rows].astype(f32), axis=0).astype(bf16)
    for z in range(copies):
        gram_ref[z] = total
    for n in range(packed_ref.shape[0]):
        lengths_ref[n : n + 1] = packed_ref[n, rows : rows + 16].astype(f32)[:1]


def recur_kernel(count, width, order, spot, sums_ref, sq_ref, *refs):
    grams = refs[: 2 * count]
    own_ref, out_ref, table, grads = refs[2 * count :]
    copies, _, t, _ = own_ref.shape
    half = count // 2

    def put(m, value):
        for z in range(copies):
            own_ref[z, m] = value

    per = count - 1
    mine = lax.rem(spot[0], 2)
    line = grams[0].shape[0]
    _, _, peers, share, r = table.shape
    for i in range(count):
        for z in range(line):
            for p in range(per):
                rows = slice(p * share, (p + 1) * share)
                table[order[i], p, 2 * z + mine] = grams[i][z, rows]
                table[order[i], p, 2 * z + 1 - mine] = grams[count + i][z, rows]
    place = {pair: n for n, pair in enumerate(gram_pairs(count))}

    def product(pair):
        n = place[pair]
        return table[n // per, n % per].reshape(peers * share, r)

    def mixed(k, l):
        return product((k, l))

    def ups(k, j, a):
        if k <= j:
            return dot(a, product((k, count + j)), 1, 0)
        return dot(a, product((j, count + k)), 1, 1)

    def total(ref, start):
        return jnp.sum(ref[:, start : start + t].astype(f32), axis=0)

    proj = [total(sums_ref, l * t) for l in range(count)]
    hu = [total(sums_ref, (count + k) * t) for k in range(count - 1)]
    back = [total(sums_ref, (2 * count - 1 + l) * t) for l in range(count)]
    norm = sq_ref[...]
    invs, pres, hus = [], [], []
    for l in range(count):
        inv = lax.rsqrt(norm / width + epsilon)
        pre = inv * proj[l]
        invs.append(inv)
        pres.append(pre)
        hus.append(list(hu))
        if l < count - 1:
            act = (pre * jax.nn.sigmoid(pre)).astype(bf16)
            put(2 + l, act)
            wide = act.astype(f32)
            for j in range(l + 1, count):
                proj[j] = proj[j] + dot(act, mixed(l, j), 1, 0)
            step = [ups(l, j, act) for j in range(count - 1)]
            norm = norm + jnp.sum(wide * (2.0 * hu[l] + step[l]), axis=-1, keepdims=True)
            hu = [hu[j] + step[j] for j in range(count - 1)]
    for l in reversed(range(count)):
        s = jax.nn.sigmoid(pres[l])
        wide = back[l] * s * (1.0 + pres[l] * (1.0 - s))
        grad = wide.astype(bf16)
        grads[l] = (wide * invs[l]).astype(bf16)
        inner = jnp.sum(wide * proj[l], axis=-1, keepdims=True) / width
        for j in range(l):
            back[j] = back[j] + invs[l] * (
                dot(grad, mixed(j, l), 1, 1) - invs[l] * invs[l] * inner * hus[l][j]
            )
    chip = order[0] // 2
    for m in range(2):
        put(m, grads[2 * chip + m])
        for j in range(1, half):
            out_ref[j - 1, m] = grads[2 * lax.rem(chip + half - j, half) + m]


def fisher_kernel(count, seqs, scale, order, place, *refs):
    half = count // 2
    rows = refs[:count]
    ups = refs[count : 2 * count]
    states = refs[2 * count : 4 * count]
    far_count = 2 * (half - 1)
    apart = refs[4 * count : 4 * count + far_count]
    rest = refs[4 * count + far_count :]
    lengths_ref, gain_ref, out_ref, acc, hidden, masks = rest
    peers, t, width = rows[0].shape
    r = out_ref.shape[1]
    chunk = min(r, width)
    span = count * t
    me = place[0]
    mine = lax.rem(place[1], 2)
    line = peers // 2
    names = [2 * (n % line) + (mine if n < line else 1 - mine) for n in range(peers)]
    spot = lax.broadcasted_iota(jnp.int32, (1, span), 1)
    position = spot
    for i in range(count):
        inside = (spot >= i * t) & (spot < (i + 1) * t)
        position = jnp.where(inside, spot + (order[i] - i) * t, position)
    position = position.astype(f32)

    def grad_rows(n, m):
        found = states[n // line * count :][:count]
        parts = []
        for i in range(count):
            core, j = divmod(i, half)
            parts.append(apart[core * (half - 1) + j - 1][names[n], m] if j else found[i][n % line, m])
        return jnp.concatenate(parts, axis=0)

    def act_rows(n, k):
        found = states[n // line * count :][:count]
        shifts = [0 if i % half else 2 for i in range(count)]
        return jnp.concatenate([found[i][n % line, shifts[i] + k] for i in range(count)], axis=0)

    acts = []
    for i in range(1, count):
        act = jnp.concatenate([act_rows(n, jnp.minimum(order[i], count - 2)) for n in range(peers)], axis=0)
        acts.append(jnp.where(order[i] < me, act, jnp.zeros_like(act)))
    for n in range(peers):
        grad = grad_rows(n, lax.rem(me, 2)).astype(f32).T
        lengths = lengths_ref[pl.ds(names[n], 1)]
        start = jnp.zeros((1, 1), f32)
        for q in range(seqs):
            stop = start + lengths[:, q : q + 1]
            inside = (position >= start) & (position < stop)
            masks[n, q * r : (q + 1) * r] = jnp.where(inside, grad, 0.0).astype(bf16)
            start = stop
    for f in range(width // chunk):
        cols = slice(f * chunk, (f + 1) * chunk)
        update = dot(acts[0], ups[1][cols], 1, 1)
        for i in range(2, count):
            update = update + dot(acts[i - 1], ups[i][cols], 1, 1)
        for n in range(peers):
            h = jnp.concatenate([rows[i][names[n], :, cols] for i in range(count)], axis=0).astype(f32)
            hidden[n] = (h + update[n * span : (n + 1) * span]).astype(bf16)
        for n in range(peers):
            total = None
            for q in range(seqs):
                g = dot(masks[n, q * r : (q + 1) * r], hidden[n], 1, 0)
                total = g * g if total is None else total + g * g
            if n == 0:
                acc[...] = total
            else:
                acc[...] = acc[...] + total
        gain = gain_ref[:, cols]
        out_ref[cols] = (acc[...] * (gain * gain * scale)).T


def per_device(tokens, cotangent, down_weight, up_weight, norm_gain, lengths):
    count = lax.axis_size("section")
    peers = lax.axis_size("dp")
    me = lax.axis_index("section")
    spot = lax.axis_index("dp")
    row_count, width = tokens.shape
    block = width // peers
    t = row_count // count
    r = down_weight.shape[2]
    order = section_order()
    smem = pl.BlockSpec(memory_space=pltpu.SMEM)
    vmem = pl.BlockSpec(memory_space=pltpu.VMEM)
    anywhere = pl.BlockSpec(memory_space=pl.ANY)

    def limit(mib):
        return pltpu.CompilerParams(vmem_limit_bytes=mib * MIB)

    place = jnp.stack([me, spot]).astype(jnp.int32)
    spot_ref = place[1:]
    ups = gather_section(up_weight[0])
    send = pl.pallas_call(
        prepare_kernel,
        out_shape=pltpu.HBM((peers, 2 * t, block), bf16),
        in_specs=[anywhere, anywhere],
        out_specs=anywhere,
        scratch_shapes=[
            pltpu.VMEM((peers, 2 * t, block), bf16),
            pltpu.SemaphoreType.DMA((2, peers)),
            pltpu.SemaphoreType.DMA((2, peers)),
        ],
        name="prepare",
    )(tokens, cotangent)
    square, weight = pl.pallas_call(
        weight_kernel,
        grid_spec=pltpu.PrefetchScalarGridSpec(
            num_scalar_prefetch=1,
            grid=(1,),
            in_specs=[
                pl.BlockSpec((peers, 2 * t, block), lambda n, place: (0, 0, 0)),
                pl.BlockSpec((1, block, r), lambda n, place: (0, 0, 0)),
                pl.BlockSpec((1, block), lambda n, place: (0, place[1])),
            ],
            out_specs=[
                pl.BlockSpec((t, 1), lambda n, place: (0, 0)),
                pl.BlockSpec((block, r), lambda n, place: (0, 0)),
            ],
        ),
        out_shape=(
            jax.ShapeDtypeStruct((t, 1), f32),
            jax.ShapeDtypeStruct((block, r), bf16),
        ),
        compiler_params=limit(12),
        name="weight",
    )(place, send, down_weight, norm_gain)
    partner = core_swap(weight)
    rows = lax.all_to_all(send, "dp", 0, 0, tiled=True)

    pairs = gram_pairs(count)
    left = lax.dynamic_slice_in_dim(jnp.array([a for a, _ in pairs], jnp.int32), me * (count - 1), count - 1)
    codes = jnp.array([b % 2 if b < count else 2 + b - count for _, b in pairs], jnp.int32)
    right = lax.dynamic_slice_in_dim(codes, me * (count - 1), count - 1)
    seqs = lengths.shape[1]
    gram_rows = (count - 1) * (r // peers)
    packed = pl.pallas_call(
        functools.partial(gram_kernel, count, seqs),
        out_shape=jax.ShapeDtypeStruct((peers, gram_rows + 16, r), bf16),
        in_specs=[smem] * 4 + [vmem] * (count + 2),
        out_specs=vmem,
        scratch_shapes=[pltpu.VMEM((2 + count, block, r), bf16)],
        compiler_params=limit(16),
        name="gram",
    )(order, left, right, lengths, *ups, weight, partner)
    packed, weight = lax.optimization_barrier((packed, weight))
    far = [chip_shift(weight, j) for j in range(1, count // 2)]

    packed = lax.all_to_all(packed, "dp", 0, 0, tiled=True)

    line = peers // 2

    def pair_shapes(blocks):
        return (
            pltpu.HBM((line, blocks * t, r), f32),
            pltpu.HBM((line, blocks * t, r), bf16),
        )

    back_keep, back_give, token_rows = pl.pallas_call(
        functools.partial(project_cot_kernel, count),
        out_shape=(*pair_shapes(count), jax.ShapeDtypeStruct((peers, t, block), bf16)),
        in_specs=[smem, smem] + [vmem] * (1 + count),
        out_specs=(vmem, vmem, vmem),
        compiler_params=limit(16),
        name="project_cot",
    )(order, spot_ref, rows, *ups)
    back_got = pair_swap(back_give)
    back_keep, *far = lax.optimization_barrier((back_keep, *far))
    downs = [weight, *far, partner, *[core_swap(b) for b in far]]
    far_rows = [chip_shift(token_rows, j) for j in range(1, count // 2)]
    keep, give = pl.pallas_call(
        functools.partial(project_kernel, count),
        out_shape=pair_shapes(2 * count - 1),
        in_specs=[smem, smem] + [vmem] * (1 + 2 * count),
        out_specs=(vmem, vmem),
        compiler_params=limit(16),
        name="project",
    )(order, spot_ref, rows, *downs, *ups)
    got, *far_rows = lax.optimization_barrier((pair_swap(give), *far_rows))
    gram_sums, all_lengths = pl.pallas_call(
        collect_kernel,
        out_shape=(pltpu.HBM((line, gram_rows, r), bf16), jax.ShapeDtypeStruct((peers, r), f32)),
        in_specs=[vmem],
        out_specs=(vmem, vmem),
        compiler_params=limit(8),
        name="collect",
    )(packed)
    gram_sums, back_got = lax.optimization_barrier((gram_sums, back_got))
    own_grams = line_exchange(gram_sums)
    part = pl.pallas_call(
        combine_kernel,
        out_shape=pltpu.HBM((line, (3 * count - 1) * t, r), bf16),
        in_specs=[vmem] * 4,
        out_specs=vmem,
        compiler_params=limit(12),
        name="combine",
    )(kept(keep, pltpu.HBM), got, kept(back_keep, pltpu.HBM), back_got)
    own_grams, part = lax.optimization_barrier((own_grams, part))
    sums = line_exchange(part)
    all_rows = [token_rows, *far_rows]
    all_rows += [core_swap(b) for b in all_rows]
    sums, all_rows = lax.optimization_barrier((sums, all_rows))
    grams = gather_section(own_grams) + gather_section(pair_swap(own_grams))

    own_held, held = pl.pallas_call(
        functools.partial(recur_kernel, count, width),
        out_shape=(
            pltpu.HBM((line, count + 1, t, r), bf16),
            pltpu.HBM((count // 2 - 1, 2, t, r), bf16),
        ),
        in_specs=[smem, smem] + [vmem] * (2 + 2 * count),
        out_specs=(vmem, vmem),
        scratch_shapes=[
            pltpu.VMEM((count, count - 1, peers, r // peers, r), bf16),
            pltpu.VMEM((count, t, r), bf16),
        ],
        compiler_params=limit(16),
        name="recur",
    )(order, spot_ref, sums, kept(square, pltpu.HBM), *[kept(g, pltpu.VMEM) for g in grams])
    gain = lax.dynamic_slice_in_dim(norm_gain, spot * block, block, 1)
    own_held, all_lengths, gain = lax.optimization_barrier((own_held, all_lengths, gain))

    half = count // 2
    own = line_exchange(own_held)
    far = [repeated(chip_shift(held[j - 1], j), peers) for j in range(1, half)]
    own, *far = lax.optimization_barrier((own, *far))
    own = [own, pair_swap(own)]
    acts = [x[:, 2:] for x in own]
    mine = [lax.all_to_all(x, "dp", 0, 0, tiled=True) for x in far]
    grads = [*mine, *[core_swap(x) for x in mine]]
    states = []
    for p in range(2):
        blocks = [own[p], *[chip_shift(acts[p], j) for j in range(1, half)]]
        states += [*blocks, *[core_swap(x) for x in blocks]]
    flat = [*states, *grads]

    chunk = min(r, block)
    fisher = pl.pallas_call(
        functools.partial(fisher_kernel, count, seqs, 1.0 / (row_count * peers)),
        out_shape=jax.ShapeDtypeStruct((block, r), f32),
        in_specs=[smem, smem] + [vmem] * (2 * count + len(flat) + 2),
        out_specs=vmem,
        scratch_shapes=[
            pltpu.VMEM((r, chunk), f32),
            pltpu.VMEM((peers, row_count, chunk), bf16),
            pltpu.VMEM((peers, seqs * r, row_count), bf16),
        ],
        compiler_params=limit(24),
        name="squares",
    )(order, place, *all_rows, *ups, *flat, all_lengths, gain)
    return fisher[None]


def solution(mesh):
    in_specs = (
        P("dp", None),
        P("dp", None),
        P("section", "dp", None),
        P("section", "dp", None),
        P("section", None),
        P("dp", None),
    )
    out_specs = P("section", "dp", None)
    return jax.shard_map(
        per_device, mesh=mesh, in_specs=in_specs, out_specs=out_specs, check_vma=False
    )
```

```python
import functools

import jax
import jax.numpy as jnp
from jax import lax
from jax.experimental import pallas as pl
from jax.experimental.pallas import tpu as pltpu
from jax.sharding import PartitionSpec as P

epsilon = 1e-05
bf16 = jnp.bfloat16
f32 = jnp.float32
MIB = 1024 * 1024


def dot(a, b, ca, cb):
    return lax.dot_general(a, b, (((ca,), (cb,)), ((), ())), preferred_element_type=f32)


def core_swap(x):
    count = lax.axis_size("section")
    return lax.ppermute(x, "section", [(i, i ^ 1) for i in range(count)])


def chip_shift(x, by):
    count = lax.axis_size("section")
    return lax.ppermute(x, "section", [(i, (i - 2 * by) % count) for i in range(count)])


def section_order():
    count = lax.axis_size("section")
    me = lax.axis_index("section")
    same = [(me + 2 * j) % count for j in range(count // 2)]
    other = [((me ^ 1) + 2 * j) % count for j in range(count // 2)]
    return jnp.stack(same + other).astype(jnp.int32)


def gather_section(x):
    count = lax.axis_size("section")
    same = [x] + [chip_shift(x, j) for j in range(1, count // 2)]
    return same + [core_swap(b) for b in same]


def kept(x, space):
    return pltpu.with_memory_space_constraint(x, space)


def pair_swap(x):
    peers = lax.axis_size("dp")
    return lax.ppermute(x, "dp", [(i, i ^ 1) for i in range(peers)])


def line_exchange(x):
    peers = lax.axis_size("dp")
    groups = [list(range(p, peers, 2)) for p in range(2)]
    return lax.all_to_all(x, "dp", 0, 0, axis_index_groups=groups, tiled=True)


def repeated(x, times):
    return jnp.broadcast_to(x[None], (times,) + x.shape)


def gram_pairs(count):
    ups = [(k, count + j) for j in range(count - 1) for k in range(j + 1)]
    listed = []
    for chip in range(count // 2):
        own = [(k, l) for l in (2 * chip, 2 * chip + 1) for k in range(l)]
        spare = 2 * (count - 1) - len(own)
        listed += own + ups[:spare]
        ups = ups[spare:]
    return listed


def prepare_kernel(tokens_ref, cot_ref, rows_ref, held, sems, out_sems):
    peers, rows, block = rows_ref.shape
    t = rows // 2
    start = pl.multiple_of(lax.axis_index("section") * t, t)
    pairs = []
    for n in range(peers):
        for k, ref in enumerate((tokens_ref, cot_ref)):
            source = ref.at[pl.ds(start, t), pl.ds(n * block, block)]
            place = (n, pl.ds(k * t, t))
            pairs.append(
                (
                    pltpu.make_async_copy(source, held.at[place], sems.at[k, n]),
                    pltpu.make_async_copy(held.at[place], rows_ref.at[place], out_sems.at[k, n]),
                )
            )
    for come, _ in pairs:
        come.start()
    for come, leave in pairs:
        come.wait()
        leave.start()
    for _, leave in pairs:
        leave.wait()


def weight_kernel(place, rows_ref, down_ref, gain_ref, square_ref, weight_ref):
    peers, rows, block = rows_ref.shape
    t = rows // 2
    total = jnp.zeros((t, 1), f32)
    for n in range(peers):
        wide = rows_ref[n, :t].astype(f32)
        total = total + jnp.sum(wide * wide, axis=-1, keepdims=True)
    square_ref[...] = total
    gain = gain_ref[...].reshape(block, 1)
    weight_ref[...] = (down_ref[0].astype(f32) * gain).astype(bf16)


def gram_kernel(count, seqs, order, left, right, lengths, *refs):
    ups = refs[:count]
    mine, partner, gram_ref, table = refs[count:]
    peers, rows, r = gram_ref.shape
    core = lax.rem(order[0], 2)
    table[core] = mine[...]
    table[1 - core] = partner[...]
    for i in range(count):
        table[2 + order[i]] = ups[i][...]
    share = r // peers
    for p in range(count - 1):
        out = dot(table[2 + left[p]], table[right[p]], 0, 0).astype(bf16)
        gram_ref[:, p * share : (p + 1) * share] = out.reshape(peers, share, r)
    used = (count - 1) * share
    lane = lax.broadcasted_iota(jnp.int32, (rows - used, r), 1)
    line = jnp.zeros((rows - used, r), f32)
    for q in range(seqs):
        line = jnp.where(lane == q, lengths[0, q].astype(f32), line)
    gram_ref[:, used:] = jnp.broadcast_to(line.astype(bf16)[None], (peers, rows - used, r))


def paired(rows, mine):
    return jnp.concatenate(rows(mine) + rows(1 - mine), axis=0)


def store_pair(keep_ref, send_ref, m, t, out):
    line, _, r = keep_ref.shape
    place = pl.ds(pl.multiple_of(m * t, t), t)
    keep_ref[:, place, :] = out[: line * t].reshape(line, t, r)
    send_ref[:, place, :] = out[line * t :].astype(bf16).reshape(line, t, r)


def project_kernel(count, order, spot, rows_ref, *refs):
    downs = refs[:count]
    ups = refs[count : 2 * count]
    keep_ref, send_ref = refs[2 * count :]
    peers, rows, _ = rows_ref.shape
    t = rows // 2
    x = paired(lambda p: [rows_ref[2 * z + p, :t] for z in range(peers // 2)], lax.rem(spot[0], 2))
    for i in range(count):
        layer = order[i]
        store_pair(keep_ref, send_ref, layer, t, dot(x, downs[i][...], 1, 0))

        @pl.when(layer < count - 1)
        def _():
            store_pair(keep_ref, send_ref, count + layer, t, dot(x, ups[i][...], 1, 0))


def project_cot_kernel(count, order, spot, rows_ref, *refs):
    ups = refs[:count]
    keep_ref, send_ref, tokens_ref = refs[count:]
    peers, rows, _ = rows_ref.shape
    t = rows // 2
    tokens_ref[...] = rows_ref[:, :t]
    c = paired(lambda p: [rows_ref[2 * z + p, t:] for z in range(peers // 2)], lax.rem(spot[0], 2))
    for i in range(count):
        store_pair(keep_ref, send_ref, order[i], t, dot(c, ups[i][...], 1, 0))


def combine_kernel(keep_ref, got_ref, back_keep_ref, back_got_ref, out_ref):
    cut = keep_ref.shape[1]
    out_ref[:, :cut] = (keep_ref[...] + got_ref[...].astype(f32)).astype(bf16)
    out_ref[:, cut:] = (back_keep_ref[...] + back_got_ref[...].astype(f32)).astype(bf16)


def collect_kernel(packed_ref, gram_ref, lengths_ref):
    copies, rows, _ = gram_ref.shape
    total = jnp.sum(packed_ref[:, :rows].astype(f32), axis=0).astype(bf16)
    for z in range(copies):
        gram_ref[z] = total
    for n in range(packed_ref.shape[0]):
        lengths_ref[n : n + 1] = packed_ref[n, rows : rows + 16].astype(f32)[:1]


def recur_kernel(count, width, order, spot, sums_ref, sq_ref, *refs):
    grams = refs[: 2 * count]
    own_ref, out_ref, table, grads = refs[2 * count :]
    copies, _, t, _ = own_ref.shape
    half = count // 2

    def put(m, value):
        for z in range(copies):
            own_ref[z, m] = value

    per = count - 1
    mine = lax.rem(spot[0], 2)
    line = grams[0].shape[0]
    _, _, peers, share, r = table.shape
    for i in range(count):
        for z in range(line):
            for p in range(per):
                rows = slice(p * share, (p + 1) * share)
                table[order[i], p, 2 * z + mine] = grams[i][z, rows]
                table[order[i], p, 2 * z + 1 - mine] = grams[count + i][z, rows]
    place = {pair: n for n, pair in enumerate(gram_pairs(count))}

    def product(pair):
        n = place[pair]
        return table[n // per, n % per].reshape(peers * share, r)

    def mixed(k, l):
        return product((k, l))

    def ups(k, j, a):
        if k <= j:
            return dot(a, product((k, count + j)), 1, 0)
        return dot(a, product((j, count + k)), 1, 1)

    def total(ref, start):
        return jnp.sum(ref[:, start : start + t].astype(f32), axis=0)

    proj = [total(sums_ref, l * t) for l in range(count)]
    hu = [total(sums_ref, (count + k) * t) for k in range(count - 1)]
    back = [total(sums_ref, (2 * count - 1 + l) * t) for l in range(count)]
    norm = sq_ref[...]
    invs, pres, hus = [], [], []
    for l in range(count):
        inv = lax.rsqrt(norm / width + epsilon)
        pre = inv * proj[l]
        invs.append(inv)
        pres.append(pre)
        hus.append(list(hu))
        if l < count - 1:
            act = (pre * jax.nn.sigmoid(pre)).astype(bf16)
            put(2 + l, act)
            wide = act.astype(f32)
            for j in range(l + 1, count):
                proj[j] = proj[j] + dot(act, mixed(l, j), 1, 0)
            step = [ups(l, j, act) for j in range(count - 1)]
            norm = norm + jnp.sum(wide * (2.0 * hu[l] + step[l]), axis=-1, keepdims=True)
            hu = [hu[j] + step[j] for j in range(count - 1)]
    for l in reversed(range(count)):
        s = jax.nn.sigmoid(pres[l])
        wide = back[l] * s * (1.0 + pres[l] * (1.0 - s))
        grad = wide.astype(bf16)
        grads[l] = (wide * invs[l]).astype(bf16)
        inner = jnp.sum(wide * proj[l], axis=-1, keepdims=True) / width
        for j in range(l):
            back[j] = back[j] + invs[l] * (
                dot(grad, mixed(j, l), 1, 1) - invs[l] * invs[l] * inner * hus[l][j]
            )
    chip = order[0] // 2
    for m in range(2):
        put(m, grads[2 * chip + m])
        for j in range(1, half):
            for n in range(out_ref.shape[1]):
                out_ref[j - 1, n, m] = grads[2 * lax.rem(chip + half - j, half) + m]


def fisher_kernel(count, seqs, scale, order, place, *refs):
    half = count // 2
    rows = refs[:count]
    ups = refs[count : 2 * count]
    states = refs[2 * count : 4 * count]
    far_count = 2 * (half - 1)
    apart = refs[4 * count : 4 * count + far_count]
    rest = refs[4 * count + far_count :]
    lengths_ref, gain_ref, out_ref, acc, hidden, masks = rest
    peers, t, width = rows[0].shape
    r = out_ref.shape[1]
    chunk = min(r, width)
    span = count * t
    me = place[0]
    mine = lax.rem(place[1], 2)
    line = peers // 2
    names = [2 * (n % line) + (mine if n < line else 1 - mine) for n in range(peers)]
    spot = lax.broadcasted_iota(jnp.int32, (1, span), 1)
    position = spot
    for i in range(count):
        inside = (spot >= i * t) & (spot < (i + 1) * t)
        position = jnp.where(inside, spot + (order[i] - i) * t, position)
    position = position.astype(f32)

    def grad_rows(n, m):
        found = states[n // line * count :][:count]
        parts = []
        for i in range(count):
            core, j = divmod(i, half)
            parts.append(apart[core * (half - 1) + j - 1][names[n], m] if j else found[i][n % line, m])
        return jnp.concatenate(parts, axis=0)

    def act_rows(n, k):
        found = states[n // line * count :][:count]
        shifts = [0 if i % half else 2 for i in range(count)]
        return jnp.concatenate([found[i][n % line, shifts[i] + k] for i in range(count)], axis=0)

    acts = []
    for i in range(1, count):
        act = jnp.concatenate([act_rows(n, jnp.minimum(order[i], count - 2)) for n in range(peers)], axis=0)
        acts.append(jnp.where(order[i] < me, act, jnp.zeros_like(act)))
    for n in range(peers):
        grad = grad_rows(n, lax.rem(me, 2)).astype(f32).T
        lengths = lengths_ref[pl.ds(names[n], 1)]
        start = jnp.zeros((1, 1), f32)
        for q in range(seqs):
            stop = start + lengths[:, q : q + 1]
            inside = (position >= start) & (position < stop)
            masks[n, q * r : (q + 1) * r] = jnp.where(inside, grad, 0.0).astype(bf16)
            start = stop
    for f in range(width // chunk):
        cols = slice(f * chunk, (f + 1) * chunk)
        update = dot(acts[0], ups[1][cols], 1, 1)
        for i in range(2, count):
            update = update + dot(acts[i - 1], ups[i][cols], 1, 1)
        for n in range(peers):
            h = jnp.concatenate([rows[i][names[n], :, cols] for i in range(count)], axis=0).astype(f32)
            hidden[n] = (h + update[n * span : (n + 1) * span]).astype(bf16)
        for n in range(peers):
            total = None
            for q in range(seqs):
                g = dot(masks[n, q * r : (q + 1) * r], hidden[n], 1, 0)
                total = g * g if total is None else total + g * g
            if n == 0:
                acc[...] = total
            else:
                acc[...] = acc[...] + total
        gain = gain_ref[:, cols]
        out_ref[cols] = (acc[...] * (gain * gain * scale)).T


def per_device(tokens, cotangent, down_weight, up_weight, norm_gain, lengths):
    count = lax.axis_size("section")
    peers = lax.axis_size("dp")
    me = lax.axis_index("section")
    spot = lax.axis_index("dp")
    row_count, width = tokens.shape
    block = width // peers
    t = row_count // count
    r = down_weight.shape[2]
    order = section_order()
    smem = pl.BlockSpec(memory_space=pltpu.SMEM)
    vmem = pl.BlockSpec(memory_space=pltpu.VMEM)
    anywhere = pl.BlockSpec(memory_space=pl.ANY)

    def limit(mib):
        return pltpu.CompilerParams(vmem_limit_bytes=mib * MIB)

    place = jnp.stack([me, spot]).astype(jnp.int32)
    spot_ref = place[1:]
    ups = gather_section(up_weight[0])
    send = pl.pallas_call(
        prepare_kernel,
        out_shape=pltpu.HBM((peers, 2 * t, block), bf16),
        in_specs=[anywhere, anywhere],
        out_specs=anywhere,
        scratch_shapes=[
            pltpu.VMEM((peers, 2 * t, block), bf16),
            pltpu.SemaphoreType.DMA((2, peers)),
            pltpu.SemaphoreType.DMA((2, peers)),
        ],
        name="prepare",
    )(tokens, cotangent)
    square, weight = pl.pallas_call(
        weight_kernel,
        grid_spec=pltpu.PrefetchScalarGridSpec(
            num_scalar_prefetch=1,
            grid=(1,),
            in_specs=[
                pl.BlockSpec((peers, 2 * t, block), lambda n, place: (0, 0, 0)),
                pl.BlockSpec((1, block, r), lambda n, place: (0, 0, 0)),
                pl.BlockSpec((1, block), lambda n, place: (0, place[1])),
            ],
            out_specs=[
                pl.BlockSpec((t, 1), lambda n, place: (0, 0)),
                pl.BlockSpec((block, r), lambda n, place: (0, 0)),
            ],
        ),
        out_shape=(
            jax.ShapeDtypeStruct((t, 1), f32),
            jax.ShapeDtypeStruct((block, r), bf16),
        ),
        compiler_params=limit(12),
        name="weight",
    )(place, send, down_weight, norm_gain)
    partner = core_swap(weight)
    rows = lax.all_to_all(send, "dp", 0, 0, tiled=True)

    pairs = gram_pairs(count)
    left = lax.dynamic_slice_in_dim(jnp.array([a for a, _ in pairs], jnp.int32), me * (count - 1), count - 1)
    codes = jnp.array([b % 2 if b < count else 2 + b - count for _, b in pairs], jnp.int32)
    right = lax.dynamic_slice_in_dim(codes, me * (count - 1), count - 1)
    seqs = lengths.shape[1]
    gram_rows = (count - 1) * (r // peers)
    packed = pl.pallas_call(
        functools.partial(gram_kernel, count, seqs),
        out_shape=jax.ShapeDtypeStruct((peers, gram_rows + 16, r), bf16),
        in_specs=[smem] * 4 + [vmem] * (count + 2),
        out_specs=vmem,
        scratch_shapes=[pltpu.VMEM((2 + count, block, r), bf16)],
        compiler_params=limit(16),
        name="gram",
    )(order, left, right, lengths, *ups, weight, partner)
    packed, weight = lax.optimization_barrier((packed, weight))
    far = [chip_shift(weight, j) for j in range(1, count // 2)]

    packed = lax.all_to_all(packed, "dp", 0, 0, tiled=True)

    line = peers // 2

    def pair_shapes(blocks):
        return (
            pltpu.HBM((line, blocks * t, r), f32),
            pltpu.HBM((line, blocks * t, r), bf16),
        )

    back_keep, back_give, token_rows = pl.pallas_call(
        functools.partial(project_cot_kernel, count),
        out_shape=(*pair_shapes(count), jax.ShapeDtypeStruct((peers, t, block), bf16)),
        in_specs=[smem, smem] + [vmem] * (1 + count),
        out_specs=(vmem, vmem, vmem),
        compiler_params=limit(16),
        name="project_cot",
    )(order, spot_ref, rows, *ups)
    back_got = pair_swap(back_give)
    back_keep, *far = lax.optimization_barrier((back_keep, *far))
    downs = [weight, *far, partner, *[core_swap(b) for b in far]]
    far_rows = [chip_shift(token_rows, j) for j in range(1, count // 2)]
    keep, give = pl.pallas_call(
        functools.partial(project_kernel, count),
        out_shape=pair_shapes(2 * count - 1),
        in_specs=[smem, smem] + [vmem] * (1 + 2 * count),
        out_specs=(vmem, vmem),
        compiler_params=limit(16),
        name="project",
    )(order, spot_ref, rows, *downs, *ups)
    got, *far_rows = lax.optimization_barrier((pair_swap(give), *far_rows))
    gram_sums, all_lengths = pl.pallas_call(
        collect_kernel,
        out_shape=(pltpu.HBM((line, gram_rows, r), bf16), jax.ShapeDtypeStruct((peers, r), f32)),
        in_specs=[vmem],
        out_specs=(vmem, vmem),
        compiler_params=limit(8),
        name="collect",
    )(packed)
    gram_sums, back_got = lax.optimization_barrier((gram_sums, back_got))
    own_grams = line_exchange(gram_sums)
    part = pl.pallas_call(
        combine_kernel,
        out_shape=pltpu.HBM((line, (3 * count - 1) * t, r), bf16),
        in_specs=[vmem] * 4,
        out_specs=vmem,
        compiler_params=limit(12),
        name="combine",
    )(kept(keep, pltpu.HBM), got, kept(back_keep, pltpu.HBM), back_got)
    own_grams, part = lax.optimization_barrier((own_grams, part))
    sums = line_exchange(part)
    all_rows = [token_rows, *far_rows]
    all_rows += [core_swap(b) for b in all_rows]
    sums, all_rows = lax.optimization_barrier((sums, all_rows))
    grams = gather_section(own_grams) + gather_section(pair_swap(own_grams))

    own_held, held = pl.pallas_call(
        functools.partial(recur_kernel, count, width),
        out_shape=(
            pltpu.HBM((line, count + 1, t, r), bf16),
            pltpu.HBM((count // 2 - 1, peers, 2, t, r), bf16),
        ),
        in_specs=[smem, smem] + [vmem] * (2 + 2 * count),
        out_specs=(vmem, vmem),
        scratch_shapes=[
            pltpu.VMEM((count, count - 1, peers, r // peers, r), bf16),
            pltpu.VMEM((count, t, r), bf16),
        ],
        compiler_params=limit(16),
        name="recur",
    )(order, spot_ref, sums, kept(square, pltpu.HBM), *[kept(g, pltpu.VMEM) for g in grams])
    gain = lax.dynamic_slice_in_dim(norm_gain, spot * block, block, 1)
    own_held, all_lengths, gain = lax.optimization_barrier((own_held, all_lengths, gain))

    half = count // 2
    own = line_exchange(own_held)
    far = [chip_shift(held[j - 1], j) for j in range(1, half)]
    own, *far = lax.optimization_barrier((own, *far))
    own = [own, pair_swap(own)]
    acts = [x[:, 2:] for x in own]
    mine = [lax.all_to_all(x, "dp", 0, 0, tiled=True) for x in far]
    grads = [*mine, *[core_swap(x) for x in mine]]
    states = []
    for p in range(2):
        blocks = [own[p], *[chip_shift(acts[p], j) for j in range(1, half)]]
        states += [*blocks, *[core_swap(x) for x in blocks]]
    flat = [*states, *grads]

    chunk = min(r, block)
    fisher = pl.pallas_call(
        functools.partial(fisher_kernel, count, seqs, 1.0 / (row_count * peers)),
        out_shape=jax.ShapeDtypeStruct((block, r), f32),
        in_specs=[smem, smem] + [vmem] * (2 * count + len(flat) + 2),
        out_specs=vmem,
        scratch_shapes=[
            pltpu.VMEM((r, chunk), f32),
            pltpu.VMEM((peers, row_count, chunk), bf16),
            pltpu.VMEM((peers, seqs * r, row_count), bf16),
        ],
        compiler_params=limit(24),
        name="squares",
    )(order, place, *all_rows, *ups, *flat, all_lengths, gain)
    return fisher[None]


def solution(mesh):
    in_specs = (
        P("dp", None),
        P("dp", None),
        P("section", "dp", None),
        P("section", "dp", None),
        P("section", None),
        P("dp", None),
    )
    out_specs = P("section", "dp", None)
    return jax.shard_map(
        per_device, mesh=mesh, in_specs=in_specs, out_specs=out_specs, check_vma=False
    )
```

```python
import functools

import jax
import jax.numpy as jnp
from jax import lax
from jax.experimental import pallas as pl
from jax.experimental.pallas import tpu as pltpu
from jax.sharding import PartitionSpec as P

epsilon = 1e-05
bf16 = jnp.bfloat16
f32 = jnp.float32
MIB = 1024 * 1024


def dot(a, b, ca, cb):
    return lax.dot_general(a, b, (((ca,), (cb,)), ((), ())), preferred_element_type=f32)


def core_swap(x):
    count = lax.axis_size("section")
    return lax.ppermute(x, "section", [(i, i ^ 1) for i in range(count)])


def chip_shift(x, by):
    count = lax.axis_size("section")
    return lax.ppermute(x, "section", [(i, (i - 2 * by) % count) for i in range(count)])


def section_order():
    count = lax.axis_size("section")
    me = lax.axis_index("section")
    same = [(me + 2 * j) % count for j in range(count // 2)]
    other = [((me ^ 1) + 2 * j) % count for j in range(count // 2)]
    return jnp.stack(same + other).astype(jnp.int32)


def gather_section(x):
    count = lax.axis_size("section")
    same = [x] + [chip_shift(x, j) for j in range(1, count // 2)]
    return same + [core_swap(b) for b in same]


def kept(x, space):
    return pltpu.with_memory_space_constraint(x, space)


def pair_swap(x):
    peers = lax.axis_size("dp")
    return lax.ppermute(x, "dp", [(i, i ^ 1) for i in range(peers)])


def line_exchange(x):
    peers = lax.axis_size("dp")
    groups = [list(range(p, peers, 2)) for p in range(2)]
    return lax.all_to_all(x, "dp", 0, 0, axis_index_groups=groups, tiled=True)


def repeated(x, times):
    return jnp.broadcast_to(x[None], (times,) + x.shape)


def gram_pairs(count):
    ups = [(k, count + j) for j in range(count - 1) for k in range(j + 1)]
    listed = []
    for chip in range(count // 2):
        own = [(k, l) for l in (2 * chip, 2 * chip + 1) for k in range(l)]
        spare = 2 * (count - 1) - len(own)
        listed += own + ups[:spare]
        ups = ups[spare:]
    return listed


def prepare_kernel(tokens_ref, cot_ref, rows_ref, held, sems, out_sems):
    peers, rows, block = rows_ref.shape
    t = rows // 2
    start = pl.multiple_of(lax.axis_index("section") * t, t)
    pairs = []
    for n in range(peers):
        for k, ref in enumerate((tokens_ref, cot_ref)):
            source = ref.at[pl.ds(start, t), pl.ds(n * block, block)]
            place = (n, pl.ds(k * t, t))
            pairs.append(
                (
                    pltpu.make_async_copy(source, held.at[place], sems.at[k, n]),
                    pltpu.make_async_copy(held.at[place], rows_ref.at[place], out_sems.at[k, n]),
                )
            )
    for come, _ in pairs:
        come.start()
    for come, leave in pairs:
        come.wait()
        leave.start()
    for _, leave in pairs:
        leave.wait()


def weight_kernel(place, rows_ref, down_ref, gain_ref, square_ref, weight_ref):
    peers, rows, block = rows_ref.shape
    t = rows // 2
    total = jnp.zeros((t, 1), f32)
    for n in range(peers):
        wide = rows_ref[n, :t].astype(f32)
        total = total + jnp.sum(wide * wide, axis=-1, keepdims=True)
    square_ref[...] = total
    gain = gain_ref[...].reshape(block, 1)
    weight_ref[...] = (down_ref[0].astype(f32) * gain).astype(bf16)


def gram_kernel(count, seqs, order, left, right, lengths, *refs):
    ups = refs[:count]
    mine, partner, gram_ref, table = refs[count:]
    peers, rows, r = gram_ref.shape
    core = lax.rem(order[0], 2)
    table[core] = mine[...]
    table[1 - core] = partner[...]
    for i in range(count):
        table[2 + order[i]] = ups[i][...]
    share = r // peers
    for p in range(count - 1):
        out = dot(table[2 + left[p]], table[right[p]], 0, 0).astype(bf16)
        gram_ref[:, p * share : (p + 1) * share] = out.reshape(peers, share, r)
    used = (count - 1) * share
    lane = lax.broadcasted_iota(jnp.int32, (rows - used, r), 1)
    line = jnp.zeros((rows - used, r), f32)
    for q in range(seqs):
        line = jnp.where(lane == q, lengths[0, q].astype(f32), line)
    gram_ref[:, used:] = jnp.broadcast_to(line.astype(bf16)[None], (peers, rows - used, r))


def paired(rows, mine):
    return jnp.concatenate(rows(mine) + rows(1 - mine), axis=0)


def store_pair(keep_ref, send_ref, m, t, out):
    line, _, r = keep_ref.shape
    place = pl.ds(pl.multiple_of(m * t, t), t)
    keep_ref[:, place, :] = out[: line * t].reshape(line, t, r)
    send_ref[:, place, :] = out[line * t :].astype(bf16).reshape(line, t, r)


def project_kernel(count, order, spot, rows_ref, *refs):
    downs = refs[:count]
    ups = refs[count : 2 * count]
    keep_ref, send_ref = refs[2 * count :]
    peers, rows, _ = rows_ref.shape
    t = rows // 2
    x = paired(lambda p: [rows_ref[2 * z + p, :t] for z in range(peers // 2)], lax.rem(spot[0], 2))
    for i in range(count):
        layer = order[i]
        store_pair(keep_ref, send_ref, layer, t, dot(x, downs[i][...], 1, 0))

        @pl.when(layer < count - 1)
        def _():
            store_pair(keep_ref, send_ref, count + layer, t, dot(x, ups[i][...], 1, 0))


def project_cot_kernel(count, order, spot, rows_ref, *refs):
    ups = refs[:count]
    keep_ref, send_ref, tokens_ref = refs[count:]
    peers, rows, _ = rows_ref.shape
    t = rows // 2
    tokens_ref[...] = rows_ref[:, :t]
    c = paired(lambda p: [rows_ref[2 * z + p, t:] for z in range(peers // 2)], lax.rem(spot[0], 2))
    for i in range(count):
        store_pair(keep_ref, send_ref, order[i], t, dot(c, ups[i][...], 1, 0))


def pair_kernel(keep_ref, got_ref, out_ref):
    out_ref[...] = (keep_ref[...] + got_ref[...].astype(f32)).astype(bf16)


def combine_kernel(keep_ref, got_ref, back_ref, out_ref):
    cut = keep_ref.shape[1]
    out_ref[:, :cut] = (keep_ref[...] + got_ref[...].astype(f32)).astype(bf16)
    out_ref[:, cut:] = back_ref[...]


def collect_kernel(packed_ref, gram_ref, lengths_ref):
    copies, rows, _ = gram_ref.shape
    total = jnp.sum(packed_ref[:, :rows].astype(f32), axis=0).astype(bf16)
    for z in range(copies):
        gram_ref[z] = total
    for n in range(packed_ref.shape[0]):
        lengths_ref[n : n + 1] = packed_ref[n, rows : rows + 8].astype(f32)[:1]


def recur_kernel(count, width, order, spot, sums_ref, sq_ref, *refs):
    grams = refs[: 2 * count]
    own_ref, out_ref, table, grads = refs[2 * count :]
    copies, _, t, _ = own_ref.shape
    half = count // 2

    def put(m, value):
        for z in range(copies):
            own_ref[z, m] = value

    per = count - 1
    mine = lax.rem(spot[0], 2)
    line = grams[0].shape[0]
    _, _, peers, share, r = table.shape
    for i in range(count):
        for z in range(line):
            for p in range(per):
                rows = slice(p * share, (p + 1) * share)
                table[order[i], p, 2 * z + mine] = grams[i][z, rows]
                table[order[i], p, 2 * z + 1 - mine] = grams[count + i][z, rows]
    place = {pair: n for n, pair in enumerate(gram_pairs(count))}

    def product(pair):
        n = place[pair]
        return table[n // per, n % per].reshape(peers * share, r)

    def mixed(k, l):
        return product((k, l))

    def ups(k, j, a):
        if k <= j:
            return dot(a, product((k, count + j)), 1, 0)
        return dot(a, product((j, count + k)), 1, 1)

    def total(ref, start):
        return jnp.sum(ref[:, start : start + t].astype(f32), axis=0)

    proj = [total(sums_ref, l * t) for l in range(count)]
    hu = [total(sums_ref, (count + k) * t) for k in range(count - 1)]
    back = [total(sums_ref, (2 * count - 1 + l) * t) for l in range(count)]
    norm = sq_ref[...]
    invs, pres, hus = [], [], []
    for l in range(count):
        inv = lax.rsqrt(norm / width + epsilon)
        pre = inv * proj[l]
        invs.append(inv)
        pres.append(pre)
        hus.append(list(hu))
        if l < count - 1:
            act = (pre * jax.nn.sigmoid(pre)).astype(bf16)
            put(2 + l, act)
            wide = act.astype(f32)
            for j in range(l + 1, count):
                proj[j] = proj[j] + dot(act, mixed(l, j), 1, 0)
            step = [ups(l, j, act) for j in range(count - 1)]
            norm = norm + jnp.sum(wide * (2.0 * hu[l] + step[l]), axis=-1, keepdims=True)
            hu = [hu[j] + step[j] for j in range(count - 1)]
    for l in reversed(range(count)):
        s = jax.nn.sigmoid(pres[l])
        wide = back[l] * s * (1.0 + pres[l] * (1.0 - s))
        grad = wide.astype(bf16)
        grads[l] = (wide * invs[l]).astype(bf16)
        inner = jnp.sum(wide * proj[l], axis=-1, keepdims=True) / width
        for j in range(l):
            back[j] = back[j] + invs[l] * (
                dot(grad, mixed(j, l), 1, 1) - invs[l] * invs[l] * inner * hus[l][j]
            )
    chip = order[0] // 2
    for m in range(2):
        put(m, grads[2 * chip + m])
        for j in range(1, half):
            for n in range(out_ref.shape[1]):
                out_ref[j - 1, n, m] = grads[2 * lax.rem(chip + half - j, half) + m]


def fisher_kernel(count, seqs, scale, order, place, *refs):
    half = count // 2
    rows = refs[:count]
    ups = refs[count : 2 * count]
    states = refs[2 * count : 4 * count]
    far_count = 2 * (half - 1)
    apart = refs[4 * count : 4 * count + far_count]
    rest = refs[4 * count + far_count :]
    lengths_ref, gain_ref, out_ref, acc, hidden, masks, held, sems = rest
    peers, t, width = rows[0].shape
    r = out_ref.shape[1]
    chunk = min(r, width)
    span = count * t
    me = place[0]
    mine = lax.rem(place[1], 2)
    line = peers // 2
    names = [2 * (n % line) + (mine if n < line else 1 - mine) for n in range(peers)]
    spot = lax.broadcasted_iota(jnp.int32, (1, span), 1)
    position = spot
    for i in range(count):
        inside = (spot >= i * t) & (spot < (i + 1) * t)
        position = jnp.where(inside, spot + (order[i] - i) * t, position)
    position = position.astype(f32)

    def grad_rows(n, m):
        found = states[n // line * count :][:count]
        parts = []
        for i in range(count):
            core, j = divmod(i, half)
            parts.append(apart[core * (half - 1) + j - 1][names[n], m] if j else found[i][n % line, m])
        return jnp.concatenate(parts, axis=0)

    def act_rows(n, k):
        found = states[n // line * count :][:count]
        shifts = [0 if i % half else 2 for i in range(count)]
        return jnp.concatenate([found[i][n % line, shifts[i] + k] for i in range(count)], axis=0)

    acts = []
    for i in range(1, count):
        act = jnp.concatenate([act_rows(n, jnp.minimum(order[i], count - 2)) for n in range(peers)], axis=0)
        acts.append(jnp.where(order[i] < me, act, jnp.zeros_like(act)))
    for n in range(peers):
        grad = grad_rows(n, lax.rem(me, 2)).astype(f32).T
        lengths = lengths_ref[pl.ds(names[n], 1)]
        start = jnp.zeros((1, 1), f32)
        for q in range(seqs):
            stop = start + lengths[:, q : q + 1]
            inside = (position >= start) & (position < stop)
            masks[n, q * r : (q + 1) * r] = jnp.where(inside, grad, 0.0).astype(bf16)
            start = stop
    copies = []
    for f in range(width // chunk):
        cols = slice(f * chunk, (f + 1) * chunk)
        update = dot(acts[0], ups[1][cols], 1, 1)
        for i in range(2, count):
            update = update + dot(acts[i - 1], ups[i][cols], 1, 1)
        for n in range(peers):
            h = jnp.concatenate([rows[i][names[n], :, cols] for i in range(count)], axis=0).astype(f32)
            hidden[n] = (h + update[n * span : (n + 1) * span]).astype(bf16)
        for n in range(peers):
            total = None
            for q in range(seqs):
                g = dot(masks[n, q * r : (q + 1) * r], hidden[n], 1, 0)
                total = g * g if total is None else total + g * g
            if n == 0:
                acc[...] = total
            else:
                acc[...] = acc[...] + total
        gain = gain_ref[:, cols]
        held[cols] = (acc[...] * (gain * gain * scale)).T
        copies.append(pltpu.make_async_copy(held.at[cols], out_ref.at[cols], sems.at[f]))
        copies[-1].start()
    for copy in copies:
        copy.wait()


def per_device(tokens, cotangent, down_weight, up_weight, norm_gain, lengths):
    count = lax.axis_size("section")
    peers = lax.axis_size("dp")
    me = lax.axis_index("section")
    spot = lax.axis_index("dp")
    row_count, width = tokens.shape
    block = width // peers
    t = row_count // count
    r = down_weight.shape[2]
    order = section_order()
    smem = pl.BlockSpec(memory_space=pltpu.SMEM)
    vmem = pl.BlockSpec(memory_space=pltpu.VMEM)
    anywhere = pl.BlockSpec(memory_space=pl.ANY)

    def limit(mib):
        return pltpu.CompilerParams(vmem_limit_bytes=mib * MIB)

    place = jnp.stack([me, spot]).astype(jnp.int32)
    spot_ref = place[1:]
    ups = gather_section(up_weight[0])
    send = pl.pallas_call(
        prepare_kernel,
        out_shape=pltpu.HBM((peers, 2 * t, block), bf16),
        in_specs=[anywhere, anywhere],
        out_specs=anywhere,
        scratch_shapes=[
            pltpu.VMEM((peers, 2 * t, block), bf16),
            pltpu.SemaphoreType.DMA((2, peers)),
            pltpu.SemaphoreType.DMA((2, peers)),
        ],
        name="prepare",
    )(tokens, cotangent)
    square, weight = pl.pallas_call(
        weight_kernel,
        grid_spec=pltpu.PrefetchScalarGridSpec(
            num_scalar_prefetch=1,
            grid=(1,),
            in_specs=[
                pl.BlockSpec((peers, 2 * t, block), lambda n, place: (0, 0, 0)),
                pl.BlockSpec((1, block, r), lambda n, place: (0, 0, 0)),
                pl.BlockSpec((1, block), lambda n, place: (0, place[1])),
            ],
            out_specs=[
                pl.BlockSpec((t, 1), lambda n, place: (0, 0)),
                pl.BlockSpec((block, r), lambda n, place: (0, 0)),
            ],
        ),
        out_shape=(
            jax.ShapeDtypeStruct((t, 1), f32),
            jax.ShapeDtypeStruct((block, r), bf16),
        ),
        compiler_params=limit(12),
        name="weight",
    )(place, send, down_weight, norm_gain)
    partner = core_swap(weight)
    rows = lax.all_to_all(send, "dp", 0, 0, tiled=True)

    pairs = gram_pairs(count)
    left = lax.dynamic_slice_in_dim(jnp.array([a for a, _ in pairs], jnp.int32), me * (count - 1), count - 1)
    codes = jnp.array([b % 2 if b < count else 2 + b - count for _, b in pairs], jnp.int32)
    right = lax.dynamic_slice_in_dim(codes, me * (count - 1), count - 1)
    seqs = lengths.shape[1]
    gram_rows = (count - 1) * (r // peers)
    packed = pl.pallas_call(
        functools.partial(gram_kernel, count, seqs),
        out_shape=jax.ShapeDtypeStruct((peers, gram_rows + 8, r), bf16),
        in_specs=[smem] * 4 + [vmem] * (count + 2),
        out_specs=vmem,
        scratch_shapes=[pltpu.VMEM((2 + count, block, r), bf16)],
        compiler_params=limit(16),
        name="gram",
    )(order, left, right, lengths, *ups, weight, partner)
    packed, weight = lax.optimization_barrier((packed, weight))
    far = [chip_shift(weight, j) for j in range(1, count // 2)]

    packed = lax.all_to_all(packed, "dp", 0, 0, tiled=True)

    line = peers // 2

    def pair_shapes(blocks):
        return (
            pltpu.HBM((line, blocks * t, r), f32),
            pltpu.HBM((line, blocks * t, r), bf16),
        )

    back_keep, back_give, token_rows = pl.pallas_call(
        functools.partial(project_cot_kernel, count),
        out_shape=(*pair_shapes(count), jax.ShapeDtypeStruct((peers, t, block), bf16)),
        in_specs=[smem, smem] + [vmem] * (1 + count),
        out_specs=(vmem, vmem, vmem),
        compiler_params=limit(16),
        name="project_cot",
    )(order, spot_ref, rows, *ups)
    back_got = pair_swap(back_give)
    back_keep, *far = lax.optimization_barrier((back_keep, *far))
    downs = [weight, *far, partner, *[core_swap(b) for b in far]]
    far_rows = [chip_shift(token_rows, j) for j in range(1, count // 2)]
    keep, give = pl.pallas_call(
        functools.partial(project_kernel, count),
        out_shape=pair_shapes(2 * count - 1),
        in_specs=[smem, smem] + [vmem] * (1 + 2 * count),
        out_specs=(vmem, vmem),
        compiler_params=limit(16),
        name="project",
    )(order, spot_ref, rows, *downs, *ups)
    got, *far_rows = lax.optimization_barrier((pair_swap(give), *far_rows))
    gram_sums, all_lengths = pl.pallas_call(
        collect_kernel,
        out_shape=(pltpu.HBM((line, gram_rows, r), bf16), jax.ShapeDtypeStruct((peers, r), f32)),
        in_specs=[vmem],
        out_specs=(vmem, vmem),
        compiler_params=limit(8),
        name="collect",
    )(packed)
    gram_sums, back_got = lax.optimization_barrier((gram_sums, back_got))
    own_grams = line_exchange(gram_sums)
    back_part = pl.pallas_call(
        pair_kernel,
        out_shape=jax.ShapeDtypeStruct((line, count * t, r), bf16),
        in_specs=[vmem] * 2,
        out_specs=vmem,
        compiler_params=limit(8),
        name="pair",
    )(kept(back_keep, pltpu.HBM), back_got)
    part = pl.pallas_call(
        combine_kernel,
        out_shape=pltpu.HBM((line, (3 * count - 1) * t, r), bf16),
        in_specs=[vmem] * 3,
        out_specs=vmem,
        compiler_params=limit(12),
        name="combine",
    )(kept(keep, pltpu.HBM), got, back_part)
    own_grams, part = lax.optimization_barrier((own_grams, part))
    sums = line_exchange(part)
    all_rows = [token_rows, *far_rows]
    all_rows += [core_swap(b) for b in all_rows]
    sums, all_rows = lax.optimization_barrier((sums, all_rows))
    grams = gather_section(own_grams) + gather_section(pair_swap(own_grams))

    own_held, held = pl.pallas_call(
        functools.partial(recur_kernel, count, width),
        out_shape=(
            pltpu.HBM((line, count + 1, t, r), bf16),
            pltpu.HBM((count // 2 - 1, peers, 2, t, r), bf16),
        ),
        in_specs=[smem, smem] + [vmem] * (2 + 2 * count),
        out_specs=(vmem, vmem),
        scratch_shapes=[
            pltpu.VMEM((count, count - 1, peers, r // peers, r), bf16),
            pltpu.VMEM((count, t, r), bf16),
        ],
        compiler_params=limit(16),
        name="recur",
    )(order, spot_ref, sums, kept(square, pltpu.HBM), *[kept(g, pltpu.VMEM) for g in grams])
    gain = lax.dynamic_slice_in_dim(norm_gain, spot * block, block, 1)
    own_held, all_lengths, gain = lax.optimization_barrier((own_held, all_lengths, gain))

    half = count // 2
    own = line_exchange(own_held)
    far = [chip_shift(held[j - 1], j) for j in range(1, half)]
    own, *far = lax.optimization_barrier((own, *far))
    own = [own, pair_swap(own)]
    acts = [x[:, 2:] for x in own]
    mine = [lax.all_to_all(x, "dp", 0, 0, tiled=True) for x in far]
    grads = [*mine, *[core_swap(x) for x in mine]]
    states = []
    for p in range(2):
        blocks = [own[p], *[chip_shift(acts[p], j) for j in range(1, half)]]
        states += [*blocks, *[core_swap(x) for x in blocks]]
    flat = [*states, *grads]

    chunk = min(r, block)
    fisher = pl.pallas_call(
        functools.partial(fisher_kernel, count, seqs, 1.0 / (row_count * peers)),
        out_shape=pltpu.HBM((block, r), f32),
        in_specs=[smem, smem] + [vmem] * (2 * count + len(flat) + 2),
        out_specs=anywhere,
        scratch_shapes=[
            pltpu.VMEM((r, chunk), f32),
            pltpu.VMEM((peers, row_count, chunk), bf16),
            pltpu.VMEM((peers, seqs * r, row_count), bf16),
            pltpu.VMEM((block, r), f32),
            pltpu.SemaphoreType.DMA((block // chunk,)),
        ],
        compiler_params=limit(24),
        name="squares",
    )(order, place, *all_rows, *ups, *flat, all_lengths, gain)
    return fisher[None]


def solution(mesh):
    in_specs = (
        P("dp", None),
        P("dp", None),
        P("section", "dp", None),
        P("section", "dp", None),
        P("section", None),
        P("dp", None),
    )
    out_specs = P("section", "dp", None)
    return jax.shard_map(
        per_device, mesh=mesh, in_specs=in_specs, out_specs=out_specs, check_vma=False
    )
```
